512 devices in a mesh: cuts: 16 (over y, x_hi, core), idx: 32 (over z, x_lo).
Axes of the slice: x: 4 (x_hi: 2, x_lo: 2; x = x_hi * 2 + x_lo), y: 4, z: 16, core: 2. Of those that a mesh axis runs over, the one named last changes fastest.
Arguments:
- boundary: bfloat16 [2, 16, 4194304], P(None, 'cuts', 'idx'), may hold values from -1.5 to 1.5
- gates_shared: bfloat16 [2, 2, 256, 256], replicated, may hold values from -0.25 to 0.25
- gates_sliced: bfloat16 [2, 16, 256, 256], P(None, 'cuts'), may hold values from -0.25 to 0.25
- cotangent: bfloat16 [2, 32, 256, 512], P(None, 'idx', 'cuts'), may hold values from -0.03125 to 0.03125
Outputs:
- amplitudes: float32 [2, 32, 256, 512], P(None, 'idx', 'cuts')
- grad_shared: float32 [2, 2, 256, 256], P(None, None, 'cuts')
- grad_sliced: float32 [2, 16, 256, 256], P(None, 'cuts')
The draws below stay inside these ranges and needn't reach their ends.
All inputs are finite; a program needn't handle non-finite values.
Results may differ from the reference program's by a relative error of at most 0.0042.
Values may be sent and summed in bfloat16 or wider, within the bound.
A program may use at most 64 MiB of HBM per device.

```python
import jax
import jax.numpy as jnp
from jax import lax

RANK = 22
SHARED = 8
MIDDLE = 5
SLICES = 16
N_IDX = 32


def block_levels(rng, extent, cuts, least, largest):
    def one(axis_at, blocks):
        heights = jax.random.uniform(jax.random.fold_in(jax.random.fold_in(rng, 6), axis_at), (blocks,), jnp.float32, least / len(cuts), largest / len(cuts))
        return jnp.repeat(jnp.exp(heights), extent[axis_at] // blocks).reshape((-1,) + (1,) * (len(extent) - axis_at - 1))

    factor_of = one(*cuts[0])
    for cut in cuts[1:]:
        factor_of = factor_of * one(*cut)
    return factor_of


def centred(own_key, shape, scale, limit, pieces=(), kind=jnp.bfloat16):
    array = scale * jax.random.normal(own_key, shape, jnp.float32)
    if pieces:
        array = array * block_levels(own_key, shape, pieces, -0.22, 0.18)
    return jnp.clip(array, -limit, limit).astype(kind)


def setup_inputs(seed: int = 0) -> dict:
    key_of = jax.random.split(jax.random.key(seed), 5)
    return {
        "boundary": centred(key_of[0], (2, SLICES, 2 ** RANK), SLICES ** -0.5, 1.5, ((1, 16), (2, 32))),
        "gates_shared": centred(key_of[1], (2, 2, 2 ** SHARED, 2 ** SHARED), (2 * 2 ** SHARED) ** -0.5, 0.25),
        "gates_sliced": centred(key_of[2], (2, SLICES, 2 ** SHARED, 2 ** SHARED), (2 * 2 ** SHARED) ** -0.5, 0.25, ((1, 16),)),
        "cotangent": centred(key_of[3], (2, N_IDX, 2 ** SHARED, 2 ** (RANK - SHARED) // N_IDX), (2 * 2 ** (RANK - SHARED)) ** -0.5, 0.03125, ((1, 32), (2, 16))),
    }


def product(left, right):
    return jnp.dot(left, right, preferred_element_type=jnp.float32, precision=lax.Precision.HIGHEST)


def rounded(values):
    return lax.optimization_barrier(values.astype(jnp.bfloat16)).astype(jnp.float32)


def gate_on(tensor, gate, positions, conjugate):
    count = len(positions)
    axes = [1 + place for place in positions]
    ends = list(range(tensor.ndim - count, tensor.ndim))
    shifted = jnp.moveaxis(tensor, axes, ends)
    shape_now = shifted.shape
    flattened = shifted.reshape(2, -1, 2 ** count)
    gate_real = gate[0]
    gate_imag = -gate[1] if conjugate else gate[1]
    real_part = product(flattened[0], gate_real) - product(flattened[1], gate_imag)
    imag_part = product(flattened[1], gate_real) + product(flattened[0], gate_imag)
    result = jnp.stack([real_part, imag_part]).reshape(shape_now)
    return jnp.moveaxis(result, ends, axes)


def grad_on(tensor, cotan, positions):
    count = len(positions)
    axes = [1 + place for place in positions]
    ends = list(range(tensor.ndim - count, tensor.ndim))
    left = jnp.moveaxis(tensor, axes, ends).reshape(2, -1, 2 ** count)
    right = jnp.moveaxis(cotan, axes, ends).reshape(2, -1, 2 ** count)
    real_part = product(left[0].T, right[0]) + product(left[1].T, right[1])
    imag_part = product(left[0].T, right[1]) - product(left[1].T, right[0])
    return jnp.stack([real_part, imag_part])


def reference(boundary, gates_shared, gates_sliced, cotangent):
    dist_bits = N_IDX.bit_length() - 1
    place_one = list(range(RANK - SHARED, RANK))
    place_two = list(range(SHARED))
    place_three = list(range(SHARED, SHARED + MIDDLE)) + list(range(RANK - SHARED + MIDDLE, RANK))
    e_axes = [1 + RANK - SHARED + number for number in range(dist_bits)]
    bit_shape = (2,) + (2,) * RANK
    cot_bits = cotangent.astype(jnp.float32).reshape((2,) + (2,) * dist_bits + (2,) * (RANK - dist_bits))
    cot_bits = jnp.moveaxis(cot_bits, list(range(1, 1 + dist_bits)), e_axes)
    gate_one = gates_shared[0].astype(jnp.float32)
    gate_two = gates_shared[1].astype(jnp.float32)

    def per_slice(carried, inputs):
        start_plane, sliced_gate = inputs
        start_tensor = start_plane.astype(jnp.float32).reshape(bit_shape)
        gate_three = sliced_gate.astype(jnp.float32)
        first_tensor = rounded(gate_on(start_tensor, gate_one, place_one, False))
        second_tensor = rounded(gate_on(first_tensor, gate_two, place_two, False))
        third_tensor = gate_on(second_tensor, gate_three, place_three, False)
        grad_three = grad_on(second_tensor, cot_bits, place_three)
        back_two = rounded(gate_on(cot_bits, jnp.swapaxes(gate_three, 1, 2), place_three, True))
        grad_two = grad_on(first_tensor, back_two, place_two)
        back_one = rounded(gate_on(back_two, jnp.swapaxes(gate_two, 1, 2), place_two, True))
        grad_one = grad_on(start_tensor, back_one, place_one)
        amp_total, shared_total = carried
        return (amp_total + third_tensor, shared_total + jnp.stack([grad_one, grad_two])), grad_three

    initial = (jnp.zeros(bit_shape, jnp.float32), jnp.zeros((2, 2, 2 ** SHARED, 2 ** SHARED), jnp.float32))
    slices_first = (jnp.moveaxis(boundary, 1, 0), jnp.moveaxis(gates_sliced, 1, 0))
    (amp_total, shared_total), sliced_all = lax.scan(per_slice, initial, slices_first)
    amplitudes = jnp.moveaxis(amp_total, e_axes, list(range(1, 1 + dist_bits))).reshape(2, N_IDX, 2 ** SHARED, -1)
    grad_sliced = jnp.moveaxis(sliced_all, 0, 1)
    return amplitudes, shared_total, grad_sliced
```

```python
import jax
import jax.numpy as jnp
from jax import lax
from jax.sharding import PartitionSpec as P


def cdot(formula, left, right, conj_left=False, conj_right=False):
    def one(a, b):
        return jnp.einsum(formula, left[a], right[b], preferred_element_type=jnp.float32)

    sl = -1.0 if conj_left else 1.0
    sr = -1.0 if conj_right else 1.0
    real = one(0, 0) - (sl * sr) * one(1, 1)
    imag = sr * one(0, 1) + sl * one(1, 0)
    return jnp.stack([real, imag])


def local(boundary, gates_shared, gates_sliced, cotangent):
    bf = jnp.bfloat16
    start = boundary.reshape(2, 8, 32, 2, 256)
    w1 = gates_shared[0].reshape(2, 256, 32, 8)
    w2 = gates_shared[1]
    w3 = gates_sliced.reshape(2, 32, 8, 32, 8)
    g3 = lax.all_to_all(cotangent[:, 0], "cuts", split_axis=2, concat_axis=1, tiled=True)
    g3b = cdot("vq,uv->uq", g3, w2, conj_right=True).astype(bf)
    g3b = g3b.reshape(2, 32, 8, 32)
    g3b = lax.all_to_all(g3b, "idx", split_axis=1, concat_axis=1, tiled=True)
    g3b = lax.all_gather(g3b, "cuts", axis=3, tiled=True)
    g3b = g3b.reshape(2, 32, 8, 32, 2, 8)
    first = cdot("lckm,med->lcked", start, w1).astype(bf)
    third = cdot("lcked,cdxy->xkyle", first, w3)
    total = lax.psum_scatter(third, "cuts", scatter_dimension=1, tiled=True).astype(bf)
    total = lax.all_to_all(total, "idx", split_axis=5, concat_axis=5, tiled=True)
    total = total.reshape(2, 32, 8, 32)
    total = total.transpose(0, 3, 2, 1).reshape(2, 256, 32)
    part = cdot("uq,uv->vq", total, w2)
    amp = lax.all_to_all(part, "cuts", split_axis=1, concat_axis=2, tiled=True)
    grad_two = cdot("uq,vq->uv", total, g3, conj_left=True)
    grad_three = cdot("lcked,elxky->cdxy", first, g3b, conj_left=True).reshape(2, 1, 256, 256)
    back_one = cdot("elxky,cdxy->lcked", g3b, w3, conj_right=True).astype(bf)
    grad_one = cdot("lckm,lcked->med", start, back_one, conj_left=True).reshape(2, 256, 256)
    shared = jnp.stack([grad_one, grad_two], axis=0)
    shared = lax.psum_scatter(shared, "cuts", scatter_dimension=2, tiled=True)
    shared, sliced = lax.psum((shared, grad_three), "idx")
    return amp[:, None], shared, sliced


def solution(mesh):
    return jax.shard_map(
        local,
        mesh=mesh,
        in_specs=(
            P(None, "cuts", "idx"),
            P(),
            P(None, "cuts", None, None),
            P(None, "idx", "cuts", None),
        ),
        out_specs=(
            P(None, "idx", "cuts", None),
            P(None, None, "cuts", None),
            P(None, "cuts", None, None),
        ),
        check_vma=False,
    )
```

```python
import jax
import jax.numpy as jnp
from jax import lax
from jax.experimental import pallas as pl
from jax.experimental.pallas import tpu as pltpu
from jax.sharding import PartitionSpec as P


BF = jnp.bfloat16
F32 = jnp.float32
MESH = pl.DeviceIdType.MESH
CUTS = 16
IDX = 32

(COT, GEX, RS1, RS2, AG1, AG2, TEX, AMP, ZS2, ZS1, N3, F3, A3, B3, NS, FS, BS, PHASES) = range(18)


def dot(a, b, contract=(1, 0)):
    return lax.dot_general(a, b, (((contract[0],), (contract[1],)), ((), ())), preferred_element_type=F32)


def selection(rows, cols, test):
    r = lax.broadcasted_iota(jnp.int32, (rows, cols), 0)
    c = lax.broadcasted_iota(jnp.int32, (rows, cols), 1)
    return jnp.where(test(r, c), 1.0, 0.0).astype(BF)


def join_lanes(pieces):
    group = lax.broadcasted_iota(jnp.int32, (32, 128), 1) >> 5
    out = None
    for j, (block, off) in enumerate(pieces):
        shift = (32 * j - off) % 128
        moved = pltpu.roll(block, shift, 1) if shift else block
        out = moved if out is None else jnp.where(group == j, moved, out)
    return out


def kernel(b_ref, ws_ref, w3_ref, cot_ref, amp_ref, gs_ref, gl_ref,
           bp, fst, xdc, xnat, w3p, cotr, gcat, grot, gsend, grecv,
           tbuf, trecv, sbuf, recv2, gt, tsend, texr, asend, arecv, bk, b1p,
           z1s, z1r, z2s, z2r, zs3, nr3, fs3, fr3, cls3, zfin,
           ss, nrs, fx, sfin, send_sem, recv_sem):
    cid = lax.axis_index("cuts")
    iid = lax.axis_index("idx")
    core, chip = cid & 1, cid >> 1
    z, xl = iid >> 1, iid & 1
    cls = ((z & 3) << 1) + xl
    far = z >> 2

    def push(phase, src, dst, **device):
        pltpu.make_async_remote_copy(
            src_ref=src, dst_ref=dst, send_sem=send_sem.at[phase], recv_sem=recv_sem.at[phase],
            device_id=device, device_id_type=MESH).start()

    def arrived(phase, ref):
        pltpu.make_async_copy(ref, ref, recv_sem.at[phase]).wait()

    def sent(phase, ref):
        pltpu.make_async_copy(ref, ref, send_sem.at[phase]).wait()

    def others(count, body):
        def step(n, carry):
            body(n)
            return carry
        lax.fori_loop(1, count, step, 0)

    barrier = pltpu.get_barrier_semaphore()
    others(CUTS, lambda n: pl.semaphore_signal(
        barrier, inc=1, device_id={"cuts": (cid + n) & (CUTS - 1)}, device_id_type=MESH))
    others(IDX, lambda n: pl.semaphore_signal(
        barrier, inc=1, device_id={"idx": (iid + n) & (IDX - 1)}, device_id_type=MESH))

    to_dc = selection(256, 256, lambda r, c: ((r >> 5) == (c & 7)) & ((r & 31) == (c >> 3)))
    from_dc = selection(256, 256, lambda r, c: ((c >> 5) == (r & 7)) & ((c & 31) == (r >> 3)))
    row_kc = selection(256, 256, lambda r, c: ((r >> 6) == (c >> 6)) & (((r >> 5) & 1) == (c & 1))
                       & ((r & 31) == ((c >> 1) & 31)))
    w1 = [dot(ws_ref[0, p], from_dc).astype(BF) for p in range(2)]
    for p in range(2):
        for h in range(2):
            rows = slice(256 * h, 256 * h + 256)
            bp[p, rows] = dot(row_kc, b_ref[p, rows]).astype(BF)

    pl.semaphore_wait(barrier, CUTS - 1 + IDX - 1)

    def quarter(c):
        return pl.ds(pl.multiple_of((c >> 2) * 128, 128), 128)

    def send_cot(n):
        to = (cid + n) & (CUTS - 1)
        push(COT, cot_ref.at[:, :, quarter(to)], cotr.at[cid], cuts=to)
    others(CUTS, send_cot)
    cotr[cid] = cot_ref[:, :, quarter(cid)]

    fst[0] = dot(bp[0], w1[0]) - dot(bp[1], w1[1])
    fst[1] = dot(bp[1], w1[0]) + dot(bp[0], w1[1])
    for p in range(2):
        for d in range(8):
            for g in range(4):
                pieces = [(fst[p, 32 * (4 * g + j):32 * (4 * g + j) + 32, 128 * (d // 4):128 * (d // 4) + 128],
                           32 * (d % 4)) for j in range(4)]
                xdc[p, 32 * d:32 * d + 32, 128 * g:128 * g + 128] = join_lanes(pieces).astype(BF)

    arrived(COT, cotr.at[pl.ds(0, CUTS - 1)])
    lane0 = (cid & 3) * 32
    s_re = selection(128, 128, lambda r, c: (c < 32) & (r == c + lane0))
    s_im = selection(128, 128, lambda r, c: (c >= 32) & (c < 64) & (r == c - 32 + lane0))
    g_re = cotr[:, 0].reshape(256, 128)
    g_im = cotr[:, 1].reshape(256, 128)
    gcat[...] = (dot(g_re, s_re) + dot(g_im, s_im)).astype(BF)
    grot[...] = (dot(g_im, s_re) - dot(g_re, s_im)).astype(BF)
    g3b = dot(ws_ref[1, 0], gcat[...]) + dot(ws_ref[1, 1], grot[...])
    gsend[...] = g3b.reshape(IDX, 8, 128)

    def send_g(n):
        to = (iid + n) & (IDX - 1)
        push(GEX, gsend.at[to], grecv.at[iid], idx=to)
    others(IDX, send_g)
    grecv[iid] = gsend[iid]

    for p in range(2):
        w3p[p] = dot(to_dc, w3_ref[p]).astype(BF)
    t_re = dot(w3p[0], xdc[0], (0, 0)) - dot(w3p[1], xdc[1], (0, 0))
    t_im = dot(w3p[0], xdc[1], (0, 0)) + dot(w3p[1], xdc[0], (0, 0))
    for c in range(CUTS):
        tbuf[c & 1, c >> 1, 0] = t_re[16 * c:16 * c + 16].astype(BF)
        tbuf[c & 1, c >> 1, 1] = t_im[16 * c:16 * c + 16].astype(BF)
    push(RS1, tbuf.at[1 - core], trecv, cuts=cid ^ 1)
    for p in range(2):
        xnat[p] = dot(from_dc, xdc[p]).astype(BF)
    arrived(RS1, trecv)
    sbuf[...] = (tbuf[core].astype(F32) + trecv[...].astype(F32)).astype(BF)

    def send_sum(n):
        to = (chip + n) & 7
        push(RS2, sbuf.at[to], recv2.at[chip], cuts=2 * to + core)
    others(8, send_sum)
    recv2[chip] = sbuf[chip]

    arrived(GEX, grecv.at[pl.ds(0, IDX - 1)])
    g_el = grecv[...].reshape(256, 128).astype(BF)
    g_own = None
    for k in range(2):
        pick = selection(128, 128, lambda r, c: (c < 32) & (r < 64) & ((r >> 4) == (c >> 3))
                         & (((r >> 3) & 1) == k) & ((r & 7) == (c & 7)))
        place = selection(256, 512, lambda r, c: ((r & 7) == (c >> 6)) & (((c >> 5) & 1) == k)
                          & ((r >> 3) == (c & 31)))
        part = dot(dot(g_el, pick).astype(BF), place, (0, 0))
        g_own = part if g_own is None else g_own + part
    gt[core, chip] = g_own[:32].astype(BF).reshape(2, 16, 512)

    def send_gather(n):
        to = (chip + n) & 7
        push(AG1, gt.at[core, chip], gt.at[core, chip], cuts=2 * to + core)
    others(8, send_gather)

    arrived(RS2, recv2.at[pl.ds(0, 7)])
    total = recv2[0].astype(F32)
    for g in range(1, 8):
        total = total + recv2[g].astype(F32)
    total = jnp.concatenate([total.reshape(32, 512).astype(BF), jnp.zeros((96, 512), BF)], axis=0)
    to_ekl = selection(512, 512, lambda r, c: ((r >> 4) == (c & 31)) & (((r >> 3) & 1) == ((c >> 5) & 1))
                       & ((r & 7) == (c >> 6)))
    tsend[...] = dot(to_ekl, total, (1, 1)).astype(BF).reshape(IDX, 16, 128)

    def send_t(n):
        to = (iid + n) & (IDX - 1)
        push(TEX, tsend.at[to], texr.at[iid], idx=to)
    others(IDX, send_t)
    texr[iid] = tsend[iid]

    arrived(AG1, gt.at[0, pl.ds(0, 7)])
    push(AG2, gt.at[core], gt.at[core], cuts=cid ^ 1)

    arrived(AG2, gt.at[0])
    gr = jnp.concatenate([gt[c & 1, c >> 1, 0] for c in range(CUTS)], axis=0)
    gi = jnp.concatenate([gt[c & 1, c >> 1, 1] for c in range(CUTS)], axis=0)
    z_re = dot(xnat[0], gr, (1, 1)) + dot(xnat[1], gi, (1, 1))
    z_im = dot(xnat[0], gi, (1, 1)) - dot(xnat[1], gr, (1, 1))
    zs3[0:4] = z_re.astype(BF).reshape(4, 64, 256)
    zs3[4:8] = z_im.astype(BF).reshape(4, 64, 256)

    def near(phase, src, dst):
        for step in (-1, 0, 1, 2):
            for flip in range(2):
                if step or flip:
                    to_z, to_x = (z + step) & 15, xl ^ flip
                    push(phase, src.at[((to_z & 3) << 1) + to_x], dst.at[2 * (step + 1) + flip], idx=2 * to_z + to_x)

    def near_back(phase, src, dst):
        for step in (-1, 0, 1, 2):
            for flip in range(2):
                if step or flip:
                    push(phase, src, dst.at[cls], idx=2 * ((z - step) & 15) + (xl ^ flip))

    near(N3, zs3, nr3)
    nr3[2] = zs3[cls]

    bk[0] = dot(w3p[0], gr) + dot(w3p[1], gi)
    bk[1] = dot(w3p[0], gi) - dot(w3p[1], gr)
    for p in range(2):
        for uk in range(16):
            for g in range(2):
                pieces = [(bk[p, 32 * (4 * g + j):32 * (4 * g + j) + 32, 128 * (uk // 4):128 * (uk // 4) + 128],
                           32 * (uk % 4)) for j in range(4)]
                b1p[p, 32 * uk:32 * uk + 32, 128 * g:128 * g + 128] = join_lanes(pieces).astype(BF)
    z_re = dot(bp[0], b1p[0], (0, 0)) + dot(bp[1], b1p[1], (0, 0))
    z_im = dot(bp[0], b1p[1], (0, 0)) - dot(bp[1], b1p[0], (0, 0))
    z1s[:, 0] = dot(z_re.astype(BF), to_dc).astype(BF).reshape(CUTS, 16, 256)
    z1s[:, 1] = dot(z_im.astype(BF), to_dc).astype(BF).reshape(CUTS, 16, 256)

    def send_cuts(phase, src, dst):
        def one(n):
            to = (cid + n) & (CUTS - 1)
            push(phase, src.at[to], dst.at[cid], cuts=to)
        others(CUTS, one)
        dst[cid] = src[cid]
    send_cuts(ZS1, z1s, z1r)

    arrived(TEX, texr.at[pl.ds(0, IDX - 1)])
    t_all = texr[...].astype(F32).reshape(IDX, 2, 8, 128)
    t_cat = t_rot = None
    for k in range(2):
        t_k = t_all[:, k].reshape(256, 128).astype(BF)
        keep = selection(128, 128, lambda r, c: (r < 32) & (c < 64) & ((r >> 3) == (c >> 4))
                         & (((c >> 3) & 1) == k) & ((r & 7) == (c & 7)))
        from_im = selection(128, 128, lambda r, c: (r >= 16) & (r < 32) & (c < 32) & (((r - 16) >> 3) == (c >> 4))
                            & (((c >> 3) & 1) == k) & ((r & 7) == (c & 7)))
        from_re = selection(128, 128, lambda r, c: (r < 16) & (c >= 32) & (c < 64) & ((r >> 3) == ((c - 32) >> 4))
                            & (((c >> 3) & 1) == k) & ((r & 7) == (c & 7)))
        one, two = dot(t_k, keep), dot(t_k, from_re) - dot(t_k, from_im)
        t_cat = one if t_cat is None else t_cat + one
        t_rot = two if t_rot is None else t_rot + two
    t_cat, t_rot = t_cat.astype(BF), t_rot.astype(BF)
    amp = dot(ws_ref[1, 0], t_cat, (0, 0)) + dot(ws_ref[1, 1], t_rot, (0, 0))
    asend[...] = amp.reshape(CUTS, 16, 128)
    send_cuts(AMP, asend, arecv)
    z2s[:, 0] = dot(t_cat, gcat[...], (1, 1)).astype(BF).reshape(CUTS, 16, 256)
    z2s[:, 1] = dot(t_cat, grot[...], (1, 1)).astype(BF).reshape(CUTS, 16, 256)
    send_cuts(ZS2, z2s, z2r)

    def add_up(ref, count):
        out = ref[0].astype(F32)
        for n in range(1, count):
            out = out + ref[n].astype(F32)
        return out

    arrived(N3, nr3.at[pl.ds(0, 7)])
    fs3[...] = add_up(nr3, 8).astype(BF).reshape(4, 16, 256)
    for hop in range(1, 4):
        to_far = (far + hop) & 3
        push(F3, fs3.at[to_far], fr3.at[far], idx=2 * (4 * to_far + (z & 3)) + xl)
    fr3[far] = fs3[far]

    arrived(ZS1, z1r.at[pl.ds(0, CUTS - 1)])
    ss[0:4] = add_up(z1r, CUTS).reshape(4, 8, 256)
    arrived(ZS2, z2r.at[pl.ds(0, CUTS - 1)])
    ss[4:8] = add_up(z2r, CUTS).reshape(4, 8, 256)
    near(NS, ss, nrs)
    nrs[2] = ss[cls]

    arrived(F3, fr3.at[pl.ds(0, 3)])
    cls3[far] = add_up(fr3, 4).astype(BF)
    for hop in range(1, 4):
        push(A3, cls3.at[far], cls3.at[far], idx=2 * (4 * ((far + hop) & 3) + (z & 3)) + xl)

    arrived(NS, nrs.at[pl.ds(0, 7)])
    fx[far] = add_up(nrs, 8)
    for hop in range(1, 4):
        push(FS, fx.at[far], fx.at[far], idx=2 * (4 * ((far + hop) & 3) + (z & 3)) + xl)

    arrived(A3, cls3.at[pl.ds(0, 3)])
    near_back(B3, cls3, zfin)
    zfin[cls] = cls3[...]

    arrived(FS, fx.at[pl.ds(0, 3)])
    sfin[cls] = add_up(fx, 4)
    near_back(BS, sfin.at[cls], sfin)

    arrived(AMP, arecv.at[pl.ds(0, CUTS - 1)])
    for p in range(2):
        for g in range(4):
            for h in range(2):
                rows = slice(8 * h, 8 * h + 8)
                group = lax.broadcasted_iota(jnp.int32, (8, 128), 1) >> 5
                out = None
                for j in range(4):
                    block = arecv[4 * g + j, rows]
                    shift = (32 * j - 32 * p) % 128
                    moved = pltpu.roll(block, shift, 1) if shift else block
                    out = moved if out is None else jnp.where(group == j, moved, out)
                amp_ref[p, rows, 128 * g:128 * g + 128] = out
    arrived(B3, zfin.at[pl.ds(0, 7)])
    for n in range(8):
        gl_ref[n // 4, 64 * (n % 4):64 * (n % 4) + 64] = zfin[n].reshape(64, 256).astype(F32)
    arrived(BS, sfin.at[pl.ds(0, 7)])
    gs_ref[...] = sfin[...].reshape(64, 256)

    sent(COT, cotr.at[pl.ds(0, CUTS - 1)])
    sent(GEX, grecv.at[pl.ds(0, IDX - 1)])
    sent(RS1, trecv)
    sent(RS2, recv2.at[pl.ds(0, 7)])
    sent(AG1, gt.at[0, pl.ds(0, 7)])
    sent(AG2, gt.at[0])
    sent(TEX, texr.at[pl.ds(0, IDX - 1)])
    sent(AMP, arecv.at[pl.ds(0, CUTS - 1)])
    sent(ZS2, z2r.at[pl.ds(0, CUTS - 1)])
    sent(ZS1, z1r.at[pl.ds(0, CUTS - 1)])
    sent(N3, nr3.at[pl.ds(0, 7)])
    sent(F3, fr3.at[pl.ds(0, 3)])
    sent(A3, cls3.at[pl.ds(0, 3)])
    sent(B3, zfin.at[pl.ds(0, 7)])
    sent(NS, nrs.at[pl.ds(0, 7)])
    sent(FS, fx.at[pl.ds(0, 3)])
    sent(BS, sfin.at[pl.ds(0, 7)])


def local(boundary, gates_shared, gates_sliced, cotangent):
    vmem = pltpu.VMEM
    scratch = [
        vmem((2, 512, 256), BF),
        vmem((2, 512, 256), F32),
        vmem((2, 256, 512), BF),
        vmem((2, 256, 512), BF),
        vmem((2, 256, 256), BF),
        vmem((CUTS, 2, 16, 128), BF),
        vmem((256, 128), BF),
        vmem((256, 128), BF),
        vmem((IDX, 8, 128), F32),
        vmem((IDX, 8, 128), F32),
        vmem((2, 8, 2, 16, 512), BF),
        vmem((8, 2, 16, 512), BF),
        vmem((8, 2, 16, 512), BF),
        vmem((8, 2, 16, 512), BF),
        vmem((2, 8, 2, 16, 512), BF),
        vmem((IDX, 16, 128), BF),
        vmem((IDX, 16, 128), BF),
        vmem((CUTS, 16, 128), F32),
        vmem((CUTS, 16, 128), F32),
        vmem((2, 256, 512), F32),
        vmem((2, 512, 256), BF),
        vmem((CUTS, 2, 16, 256), BF),
        vmem((CUTS, 2, 16, 256), BF),
        vmem((CUTS, 2, 16, 256), BF),
        vmem((CUTS, 2, 16, 256), BF),
        vmem((8, 64, 256), BF),
        vmem((8, 64, 256), BF),
        vmem((4, 16, 256), BF),
        vmem((4, 16, 256), BF),
        vmem((4, 16, 256), BF),
        vmem((8, 4, 16, 256), BF),
        vmem((8, 8, 256), F32),
        vmem((8, 8, 256), F32),
        vmem((4, 8, 256), F32),
        vmem((8, 8, 256), F32),
        pltpu.SemaphoreType.DMA((PHASES,)),
        pltpu.SemaphoreType.DMA((PHASES,)),
    ]
    amp, shared, sliced = pl.pallas_call(
        kernel,
        out_shape=(
            jax.ShapeDtypeStruct((2, 16, 512), F32),
            jax.ShapeDtypeStruct((64, 256), F32),
            jax.ShapeDtypeStruct((2, 256, 256), F32),
        ),
        in_specs=[pl.BlockSpec(memory_space=vmem)] * 4,
        out_specs=[pl.BlockSpec(memory_space=vmem)] * 3,
        scratch_shapes=scratch,
        compiler_params=pltpu.CompilerParams(
            collective_id=0, has_side_effects=True, vmem_limit_bytes=40 * 2 ** 20),
    )(boundary.reshape(2, 512, 256), gates_shared, gates_sliced[:, 0], cotangent[:, 0])
    return amp[:, None], shared.reshape(2, 2, 16, 256), sliced[:, None]


def solution(mesh):
    return jax.shard_map(
        local,
        mesh=mesh,
        in_specs=(
            P(None, "cuts", "idx"),
            P(),
            P(None, "cuts", None, None),
            P(None, "idx", "cuts", None),
        ),
        out_specs=(
            P(None, "idx", "cuts", None),
            P(None, None, "cuts", None),
            P(None, "cuts", None, None),
        ),
        check_vma=False,
    )
```

```python
import jax
import jax.numpy as jnp
from jax import lax
from jax.experimental import pallas as pl
from jax.experimental.pallas import tpu as pltpu
from jax.sharding import PartitionSpec as P


BF = jnp.bfloat16
F32 = jnp.float32
MESH = pl.DeviceIdType.MESH
CUTS = 16

(COT, GEX, RS1, RS2, AG1, AG2, TEX, AMP, ZS2, ZS1, N3A, N3B, F3, B3, NS, FS, BS, PHASES) = range(18)

LINE = sorted(range(1, 16), key=lambda n: -min(n, 16 - n))
NEAR = [(2, 1), (2, 0), (-1, 1), (1, 1), (-1, 0), (1, 0), (0, 1)]


def hops(dy, dx, dc, flip):
    return min(dy, 4 - dy) + (2 if dx > flip else max(dx, flip)) + 0.5 * dc


CUT_STEPS = sorted(((dy, dx, dc) for dy in range(4) for dx in range(2) for dc in range(2) if dy + dx + dc),
                   key=lambda t: -hops(*t, 0))
PLANE_STEPS = sorted(((dy, dx, flip) for dy in range(4) for dx in range(2) for flip in range(2) if dy + dx + flip),
                     key=lambda t: -hops(t[0], t[1], 0, t[2]))


def dot(a, b, contract=(1, 0)):
    return lax.dot_general(a, b, (((contract[0],), (contract[1],)), ((), ())), preferred_element_type=F32)


def selection(rows, cols, test):
    r = lax.broadcasted_iota(jnp.int32, (rows, cols), 0)
    c = lax.broadcasted_iota(jnp.int32, (rows, cols), 1)
    return jnp.where(test(r, c), 1.0, 0.0).astype(BF)


def join_lanes(pieces):
    group = lax.broadcasted_iota(jnp.int32, (32, 128), 1) >> 5
    out = None
    for j, (block, off) in enumerate(pieces):
        shift = (32 * j - off) % 128
        moved = pltpu.roll(block, shift, 1) if shift else block
        out = moved if out is None else jnp.where(group == j, moved, out)
    return out


def kernel(b_ref, ws_ref, w3_ref, cot_ref, amp_ref, gs_ref, gl_ref,
           bp, fst, xdc, xp, xnat, w3p, cotr, gcat, grot, gsend, grecv, gown,
           tbuf, trecv, sbuf, recv2, gt, tsend, texr, asend, arecv, bk, b1p,
           z1s, z1r, z2s, z2r, zs3, nr3, clsx, cls3, zfin,
           ss, nrs, fx, sfin, send_sem, recv_sem):
    cid = lax.axis_index("cuts")
    iid = lax.axis_index("idx")
    y, xh, core, chip = cid >> 2, (cid >> 1) & 1, cid & 1, cid >> 1
    z, xl = iid >> 1, iid & 1
    cls = ((z & 3) << 1) + xl
    far = z >> 2

    totals = {
        COT: cotr.at[pl.ds(0, 15)], GEX: grecv.at[pl.ds(0, 15)], RS1: trecv, RS2: recv2.at[pl.ds(0, 15)],
        AG1: gt.at[0, pl.ds(0, 15)], AG2: gt.at[0], TEX: texr.at[pl.ds(0, 15)], AMP: arecv.at[pl.ds(0, 15)],
        ZS2: z2r.at[pl.ds(0, 15)], ZS1: z1r.at[pl.ds(0, 15)], N3A: nr3.at[0, pl.ds(0, 7)],
        N3B: nr3.at[0, pl.ds(0, 7)], F3: clsx.at[pl.ds(0, 3)], B3: zfin.at[pl.ds(0, 7)],
        NS: nrs.at[pl.ds(0, 7)], FS: fx.at[pl.ds(0, 3)], BS: sfin.at[pl.ds(0, 7)]}
    started = []

    def push(phase, src, dst, cuts=None, idx=None):
        if phase not in started:
            started.append(phase)
        device = {}
        if cuts is not None:
            device["cuts"] = cuts
        if idx is not None:
            device["idx"] = idx
        pltpu.make_async_remote_copy(
            src_ref=src, dst_ref=dst, send_sem=send_sem.at[phase], recv_sem=recv_sem.at[phase],
            device_id=device, device_id_type=MESH).start()

    def arrived(phase):
        pltpu.make_async_copy(totals[phase], totals[phase], recv_sem.at[phase]).wait()

    def chip_at(dy, dx):
        return (((y + dy) & 3) << 1) + (xh ^ dx)

    barrier = pltpu.get_barrier_semaphore()

    def greet(**device):
        pl.semaphore_signal(barrier, inc=1, device_id=device, device_id_type=MESH)
    for n in LINE:
        greet(idx=2 * ((z + n) & 15) + xl)
    for n in (2, 14, 1, 15):
        greet(idx=2 * ((z + n) & 15) + (xl ^ 1))
    for dy, dx, dc in CUT_STEPS:
        greet(cuts=2 * chip_at(dy, dx) + (core ^ dc))
    for dy in range(4):
        for dx in range(2):
            greet(cuts=2 * chip_at(dy, dx) + core, idx=iid ^ 1)

    to_dc = selection(256, 256, lambda r, c: ((r >> 5) == (c & 7)) & ((r & 31) == (c >> 3)))
    from_dc = selection(256, 256, lambda r, c: ((c >> 5) == (r & 7)) & ((c & 31) == (r >> 3)))
    row_kc = selection(256, 256, lambda r, c: ((r >> 6) == (c >> 6)) & (((r >> 5) & 1) == (c & 1))
                       & ((r & 31) == ((c >> 1) & 31)))
    to_xlkz = selection(512, 512, lambda r, c: ((r & 1) == (c >> 8)) & (((r >> 1) & 15) == (c & 15))
                        & (((r >> 5) & 1) == ((c >> 4) & 1)) & ((r >> 6) == ((c >> 5) & 7)))

    pl.semaphore_wait(barrier, 42)

    def quarter(c):
        return pl.ds(pl.multiple_of((c >> 2) * 128, 128), 128)

    for dy, dx, dc in CUT_STEPS:
        to = 2 * chip_at(dy, dx) + (core ^ dc)
        push(COT, cot_ref.at[:, :, quarter(to)], cotr.at[cid], cuts=to)
    cotr[cid] = cot_ref[:, :, quarter(cid)]

    w1 = [dot(ws_ref[0, p], from_dc).astype(BF) for p in range(2)]
    for p in range(2):
        for h in range(2):
            rows = slice(256 * h, 256 * h + 256)
            bp[p, rows] = dot(row_kc, b_ref[p, rows]).astype(BF)
    fst[0] = dot(bp[0], w1[0]) - dot(bp[1], w1[1])
    fst[1] = dot(bp[1], w1[0]) + dot(bp[0], w1[1])
    for p in range(2):
        for d in range(8):
            for g in range(4):
                pieces = [(fst[p, 32 * (4 * g + j):32 * (4 * g + j) + 32, 128 * (d // 4):128 * (d // 4) + 128],
                           32 * (d % 4)) for j in range(4)]
                xdc[p, 32 * d:32 * d + 32, 128 * g:128 * g + 128] = join_lanes(pieces).astype(BF)
        xp[p] = dot(xdc[p], to_xlkz).astype(BF)

    for p in range(2):
        w3p[p] = dot(to_dc, w3_ref[p]).astype(BF)
    t_re = dot(w3p[0], xp[0], (0, 0)) - dot(w3p[1], xp[1], (0, 0))
    t_im = dot(w3p[0], xp[1], (0, 0)) + dot(w3p[1], xp[0], (0, 0))
    for c in range(CUTS):
        for x in range(2):
            rows, lanes = slice(16 * c, 16 * c + 16), slice(256 * x, 256 * x + 256)
            tbuf[c & 1, 8 * x + (c >> 1), 0] = t_re[rows, lanes].astype(BF)
            tbuf[c & 1, 8 * x + (c >> 1), 1] = t_im[rows, lanes].astype(BF)
    push(RS1, tbuf.at[1 - core], trecv, cuts=cid ^ 1)
    for p in range(2):
        xnat[p] = dot(from_dc, xp[p]).astype(BF)
    arrived(RS1)
    sbuf[...] = (tbuf[core].astype(F32) + trecv[...].astype(F32)).astype(BF)
    for dy, dx, flip in PLANE_STEPS:
        to, to_x = chip_at(dy, dx), xl ^ flip
        push(RS2, sbuf.at[8 * to_x + to], recv2.at[8 * xl + chip], cuts=2 * to + core, idx=2 * z + to_x)
    recv2[8 * xl + chip] = sbuf[8 * xl + chip]

    arrived(COT)
    lane0 = (cid & 3) * 32
    s_re = selection(128, 128, lambda r, c: (c < 32) & (r == c + lane0))
    s_im = selection(128, 128, lambda r, c: (c >= 32) & (c < 64) & (r == c - 32 + lane0))
    g_re = cotr[:, 0].reshape(256, 128)
    g_im = cotr[:, 1].reshape(256, 128)
    gcat[...] = (dot(g_re, s_re) + dot(g_im, s_im)).astype(BF)
    grot[...] = (dot(g_im, s_re) - dot(g_re, s_im)).astype(BF)
    g3b = dot(ws_ref[1, 0], gcat[...]) + dot(ws_ref[1, 1], grot[...])
    gsend[...] = g3b.astype(BF).reshape(16, 16, 128)
    for n in LINE:
        to = (z + n) & 15
        push(GEX, gsend.at[to], grecv.at[z], idx=2 * to + xl)
    grecv[z] = gsend[z]

    arrived(RS2)
    rows = []
    for x in range(2):
        part = recv2[8 * x].astype(F32)
        for g in range(1, 8):
            part = part + recv2[8 * x + g].astype(F32)
        rows.append(part.reshape(32, 256).astype(BF))
    rows.append(jnp.zeros((64, 256), BF))
    to_zkl = selection(256, 256, lambda r, c: ((r >> 4) == (c & 15)) & (((r >> 3) & 1) == ((c >> 4) & 1))
                       & ((r & 7) == (c >> 5)))
    tsend[...] = dot(to_zkl, jnp.concatenate(rows, axis=0), (1, 1)).astype(BF).reshape(16, 16, 128)
    for n in LINE:
        to = (z + n) & 15
        push(TEX, tsend.at[to], texr.at[z], idx=2 * to + xl)
    texr[z] = tsend[z]

    arrived(GEX)
    g_all = grecv[...].astype(F32).reshape(16, 2, 8, 128)
    for x in range(2):
        g_zl = g_all[:, x].reshape(128, 128).astype(BF)
        out = None
        for k in range(2):
            pick = selection(128, 128, lambda r, c: (c < 32) & (r < 64) & ((r >> 4) == (c >> 3))
                             & (((r >> 3) & 1) == k) & ((r & 7) == (c & 7)))
            place = selection(128, 256, lambda r, c: ((r & 7) == (c >> 5)) & (((c >> 4) & 1) == k)
                              & ((r >> 3) == (c & 15)))
            part = dot(dot(g_zl, pick).astype(BF), place, (0, 0))
            out = part if out is None else out + part
        gown[x] = out[:32].astype(BF).reshape(2, 16, 256)
    for dy, dx, flip in PLANE_STEPS:
        to_x = xl ^ flip
        push(AG1, gown.at[to_x], gt.at[core, 2 * chip + xl], cuts=2 * chip_at(dy, dx) + core, idx=2 * z + to_x)
    gt[core, 2 * chip + xl] = gown[xl]

    def push_cuts(phase, src, dst):
        for dy, dx, dc in CUT_STEPS:
            to = 2 * chip_at(dy, dx) + (core ^ dc)
            push(phase, src.at[to], dst.at[cid], cuts=to)
        dst[cid] = src[cid]

    arrived(TEX)
    t_all = texr[...].astype(F32).reshape(16, 2, 8, 128)
    t_k = [t_all[:, k].reshape(128, 128).astype(BF) for k in range(2)]
    cat, rot = [], []
    for x in range(2):
        one = two = None
        for k in range(2):
            def same(r, c):
                return (c < 64) & ((r >> 5) == x) & (((c >> 3) & 1) == k) & ((r & 7) == (c & 7)) \
                    & (((r >> 3) & 1) == ((c >> 4) & 1))
            keep = selection(128, 128, lambda r, c: same(r, c) & (((r >> 4) & 1) == (c >> 5)))
            to_im = selection(128, 128, lambda r, c: same(r, c) & (((r >> 4) & 1) == 0) & (c >= 32))
            to_re = selection(128, 128, lambda r, c: same(r, c) & (((r >> 4) & 1) == 1) & (c < 32))
            a, b = dot(t_k[k], keep), dot(t_k[k], to_im - to_re)
            one, two = (a, b) if one is None else (one + a, two + b)
        cat.append(one.astype(BF))
        rot.append(two.astype(BF))
    to_u = selection(256, 256, lambda r, c: ((r >> 4) == ((c >> 3) & 15)) & (((r >> 3) & 1) == (c >> 7))
                     & ((r & 7) == (c & 7)))
    t_cat = dot(to_u, jnp.concatenate(cat, axis=0)).astype(BF)
    t_rot = dot(to_u, jnp.concatenate(rot, axis=0)).astype(BF)
    amp = dot(ws_ref[1, 0], t_cat, (0, 0)) + dot(ws_ref[1, 1], t_rot, (0, 0))
    asend[...] = amp.reshape(CUTS, 16, 128)
    z2s[:, 0] = dot(t_cat, gcat[...], (1, 1)).astype(BF).reshape(CUTS, 16, 256)
    z2s[:, 1] = dot(t_cat, grot[...], (1, 1)).astype(BF).reshape(CUTS, 16, 256)
    push_cuts(ZS2, z2s, z2r)
    push_cuts(AMP, asend, arecv)

    def near(phase, src, dst):
        for step, flip in NEAR:
            to_z, to_x = (z + step) & 15, xl ^ flip
            push(phase, src.at[((to_z & 3) << 1) + to_x], dst.at[2 * (step + 1) + flip], idx=2 * to_z + to_x)
        dst[2] = src[cls]

    def near_back(phase, src, dst):
        for step, flip in NEAR:
            push(phase, src, dst.at[cls], idx=2 * ((z - step) & 15) + (xl ^ flip))

    def grad_three(half, phase):
        g = [jnp.concatenate([jnp.concatenate([gt[half, 2 * n, p], gt[half, 2 * n + 1, p]], axis=1)
                              for n in range(8)], axis=0) for p in range(2)]
        z_re = dot(xnat[0], g[0], (1, 1)) + dot(xnat[1], g[1], (1, 1))
        z_im = dot(xnat[0], g[1], (1, 1)) - dot(xnat[1], g[0], (1, 1))
        zs3[half, 0:4] = z_re.astype(BF).reshape(4, 64, 128)
        zs3[half, 4:8] = z_im.astype(BF).reshape(4, 64, 128)
        near(phase, zs3.at[half], nr3.at[half])

    arrived(AG1)
    push(AG2, gt.at[core], gt.at[core], cuts=cid ^ 1)
    grad_three(core, N3A)
    arrived(AG2)
    grad_three(1 - core, N3B)

    gr, gi = [
        dot(jnp.concatenate([jnp.concatenate([gt[c & 1, 2 * (c >> 1), p], gt[c & 1, 2 * (c >> 1) + 1, p]], axis=1)
                             for c in range(CUTS)], axis=0), to_xlkz, (1, 1)).astype(BF) for p in range(2)]
    bk[0] = dot(w3p[0], gr) + dot(w3p[1], gi)
    bk[1] = dot(w3p[0], gi) - dot(w3p[1], gr)
    for p in range(2):
        for uk in range(16):
            for g in range(2):
                pieces = [(bk[p, 32 * (4 * g + j):32 * (4 * g + j) + 32, 128 * (uk // 4):128 * (uk // 4) + 128],
                           32 * (uk % 4)) for j in range(4)]
                b1p[p, 32 * uk:32 * uk + 32, 128 * g:128 * g + 128] = join_lanes(pieces).astype(BF)
    z_re = dot(bp[0], b1p[0], (0, 0)) + dot(bp[1], b1p[1], (0, 0))
    z_im = dot(bp[0], b1p[1], (0, 0)) - dot(bp[1], b1p[0], (0, 0))
    z1s[:, 0] = dot(z_re.astype(BF), to_dc).astype(BF).reshape(CUTS, 16, 256)
    z1s[:, 1] = dot(z_im.astype(BF), to_dc).astype(BF).reshape(CUTS, 16, 256)
    push_cuts(ZS1, z1s, z1r)

    def add_up(ref, count):
        out = ref[0].astype(F32)
        for n in range(1, count):
            out = out + ref[n].astype(F32)
        return out

    def push_far(phase, ref):
        for hop in (2, 1, 3):
            push(phase, ref.at[far], ref.at[far], idx=2 * (4 * ((far + hop) & 3) + (z & 3)) + xl)

    arrived(N3A)
    arrived(N3B)
    for half in range(2):
        clsx[far, half] = add_up(nr3.at[half], 8).astype(BF)
    push_far(F3, clsx)

    arrived(ZS2)
    ss[4:8] = add_up(z2r, CUTS).reshape(4, 8, 256)
    arrived(ZS1)
    ss[0:4] = add_up(z1r, CUTS).reshape(4, 8, 256)
    near(NS, ss, nrs)

    arrived(F3)
    cls3[...] = add_up(clsx, 4).astype(BF)
    near_back(B3, cls3, zfin)
    zfin[cls] = cls3[...]

    arrived(NS)
    fx[far] = add_up(nrs, 8)
    push_far(FS, fx)

    arrived(AMP)
    group = lax.broadcasted_iota(jnp.int32, (8, 128), 1) >> 5
    for p in range(2):
        for g in range(4):
            for h in range(2):
                rows = slice(8 * h, 8 * h + 8)
                out = None
                for j in range(4):
                    block = arecv[4 * g + j, rows]
                    shift = (32 * j - 32 * p) % 128
                    moved = pltpu.roll(block, shift, 1) if shift else block
                    out = moved if out is None else jnp.where(group == j, moved, out)
                amp_ref[p, rows, 128 * g:128 * g + 128] = out

    arrived(FS)
    sfin[cls] = add_up(fx, 4)
    near_back(BS, sfin.at[cls], sfin)

    to_cut = selection(256, 256, lambda r, c: ((r >> 7) == ((c >> 4) & 1)) & (((r >> 4) & 7) == (c >> 5))
                       & ((r & 15) == (c & 15)))
    arrived(B3)
    for n in range(8):
        block = jnp.concatenate([zfin[n, 0], zfin[n, 1]], axis=1)
        gl_ref[n // 4, 64 * (n % 4):64 * (n % 4) + 64] = dot(block, to_cut)
    arrived(BS)
    gs_ref[...] = sfin[...].reshape(64, 256)

    for phase in started:
        pltpu.make_async_copy(totals[phase], totals[phase], send_sem.at[phase]).wait()


def local(boundary, gates_shared, gates_sliced, cotangent):
    vmem = pltpu.VMEM
    scratch = [
        vmem((2, 512, 256), BF),
        vmem((2, 512, 256), F32),
        vmem((2, 256, 512), BF),
        vmem((2, 256, 512), BF),
        vmem((2, 256, 512), BF),
        vmem((2, 256, 256), BF),
        vmem((CUTS, 2, 16, 128), BF),
        vmem((256, 128), BF),
        vmem((256, 128), BF),
        vmem((16, 16, 128), BF),
        vmem((16, 16, 128), BF),
        vmem((2, 2, 16, 256), BF),
        vmem((2, 16, 2, 16, 256), BF),
        vmem((16, 2, 16, 256), BF),
        vmem((16, 2, 16, 256), BF),
        vmem((16, 2, 16, 256), BF),
        vmem((2, 16, 2, 16, 256), BF),
        vmem((16, 16, 128), BF),
        vmem((16, 16, 128), BF),
        vmem((CUTS, 16, 128), F32),
        vmem((CUTS, 16, 128), F32),
        vmem((2, 256, 512), F32),
        vmem((2, 512, 256), BF),
        vmem((CUTS, 2, 16, 256), BF),
        vmem((CUTS, 2, 16, 256), BF),
        vmem((CUTS, 2, 16, 256), BF),
        vmem((CUTS, 2, 16, 256), BF),
        vmem((2, 8, 64, 128), BF),
        vmem((2, 8, 64, 128), BF),
        vmem((4, 2, 64, 128), BF),
        vmem((2, 64, 128), BF),
        vmem((8, 2, 64, 128), BF),
        vmem((8, 8, 256), F32),
        vmem((8, 8, 256), F32),
        vmem((4, 8, 256), F32),
        vmem((8, 8, 256), F32),
        pltpu.SemaphoreType.DMA((PHASES,)),
        pltpu.SemaphoreType.DMA((PHASES,)),
    ]
    amp, shared, sliced = pl.pallas_call(
        kernel,
        out_shape=(
            jax.ShapeDtypeStruct((2, 16, 512), F32),
            jax.ShapeDtypeStruct((64, 256), F32),
            jax.ShapeDtypeStruct((2, 256, 256), F32),
        ),
        in_specs=[pl.BlockSpec(memory_space=vmem)] * 4,
        out_specs=[pl.BlockSpec(memory_space=vmem)] * 3,
        scratch_shapes=scratch,
        compiler_params=pltpu.CompilerParams(
            collective_id=0, has_side_effects=True, vmem_limit_bytes=40 * 2 ** 20),
    )(boundary.reshape(2, 512, 256), gates_shared, gates_sliced[:, 0], cotangent[:, 0])
    return amp[:, None], shared.reshape(2, 2, 16, 256), sliced[:, None]


def solution(mesh):
    return jax.shard_map(
        local,
        mesh=mesh,
        in_specs=(
            P(None, "cuts", "idx"),
            P(),
            P(None, "cuts", None, None),
            P(None, "idx", "cuts", None),
        ),
        out_specs=(
            P(None, "idx", "cuts", None),
            P(None, None, "cuts", None),
            P(None, "cuts", None, None),
        ),
        check_vma=False,
    )
```

```python
import jax
import jax.numpy as jnp
from jax import lax
from jax.experimental import pallas as pl
from jax.experimental.pallas import tpu as pltpu
from jax.sharding import PartitionSpec as P


BF = jnp.bfloat16
F32 = jnp.float32
MESH = pl.DeviceIdType.MESH
CUTS = 16

(COT, GEX, RS1, RS2, AG1, AG2, TEX, ZS2, ZS1, NS, FS, BS, N3, F3, B3) = range(15)
PHASES = 18

LINE = sorted(range(1, 16), key=lambda n: -min(n, 16 - n))
NEAR = [(2, 1), (2, 0), (-1, 1), (1, 1), (-1, 0), (1, 0), (0, 1)]


def hops(dy, dx, dc, flip):
    return min(dy, 4 - dy) + (2 if dx > flip else max(dx, flip)) + 0.5 * dc


CUT_STEPS = sorted(((dy, dx, dc) for dy in range(4) for dx in range(2) for dc in range(2) if dy + dx + dc),
                   key=lambda t: -hops(*t, 0))
PLANE_STEPS = sorted(((dy, dx, flip) for dy in range(4) for dx in range(2) for flip in range(2) if dy + dx + flip),
                     key=lambda t: -hops(t[0], t[1], 0, t[2]))


def dot(a, b, contract=(1, 0)):
    return lax.dot_general(a, b, (((contract[0],), (contract[1],)), ((), ())), preferred_element_type=F32)


def selection(rows, cols, test):
    r = lax.broadcasted_iota(jnp.int32, (rows, cols), 0)
    c = lax.broadcasted_iota(jnp.int32, (rows, cols), 1)
    return jnp.where(test(r, c), 1.0, 0.0).astype(BF)


def join_lanes(pieces):
    group = lax.broadcasted_iota(jnp.int32, (32, 128), 1) >> 5
    out = None
    for j, (block, off) in enumerate(pieces):
        shift = (32 * j - off) % 128
        moved = pltpu.roll(block, shift, 1) if shift else block
        out = moved if out is None else jnp.where(group == j, moved, out)
    return out


def kernel(b_ref, ws_ref, w3_ref, cot_ref, amp_ref, gs_ref, gl_ref,
           bp, fst, xdc, xp, xnat, w3p, cotr, gcat, grot, gsend, grecv, gown,
           tbuf, trecv, sbuf, recv2, gt, tsend, texr, bk, b1p,
           z1s, z1r, z2s, z2r, zs3, nr3, clsx, cls3, zfin,
           ss, nrs, fx, sfin, send_sem, recv_sem):
    cid = lax.axis_index("cuts")
    iid = lax.axis_index("idx")
    y, xh, core, chip = cid >> 2, (cid >> 1) & 1, cid & 1, cid >> 1
    z, xl = iid >> 1, iid & 1
    cls = ((z & 3) << 1) + xl
    far = z >> 2

    totals = {
        COT: cotr.at[pl.ds(0, 15)], GEX: grecv.at[pl.ds(0, 15)], RS1: trecv, RS2: recv2.at[pl.ds(0, 15)],
        AG1: gt.at[0, pl.ds(0, 15)], AG2: gt.at[0], TEX: texr.at[pl.ds(0, 15)],
        ZS2: z2r.at[pl.ds(0, 15)], ZS1: z1r.at[pl.ds(0, 15)], NS: nrs.at[pl.ds(0, 7)], FS: fx.at[pl.ds(0, 3)], BS: sfin.at[pl.ds(0, 7)]}
    for part in (0, 3):
        totals[N3 + part] = nr3.at[0, pl.ds(0, 7)]
        totals[F3 + part] = clsx.at[0, pl.ds(0, 3)]
        totals[B3 + part] = zfin.at[0, pl.ds(0, 7)]
    started = []

    def push(phase, src, dst, cuts=None, idx=None):
        if phase not in started:
            started.append(phase)
        device = {}
        if cuts is not None:
            device["cuts"] = cuts
        if idx is not None:
            device["idx"] = idx
        pltpu.make_async_remote_copy(
            src_ref=src, dst_ref=dst, send_sem=send_sem.at[phase], recv_sem=recv_sem.at[phase],
            device_id=device, device_id_type=MESH).start()

    def arrived(phase):
        pltpu.make_async_copy(totals[phase], totals[phase], recv_sem.at[phase]).wait()

    def chip_at(dy, dx):
        return (((y + dy) & 3) << 1) + (xh ^ dx)

    barrier = pltpu.get_barrier_semaphore()

    def greet(**device):
        pl.semaphore_signal(barrier, inc=1, device_id=device, device_id_type=MESH)
    for n in LINE:
        greet(idx=2 * ((z + n) & 15) + xl)
    for n in (2, 14, 1, 15):
        greet(idx=2 * ((z + n) & 15) + (xl ^ 1))
    for dy, dx, dc in CUT_STEPS:
        greet(cuts=2 * chip_at(dy, dx) + (core ^ dc))
    for dy in range(4):
        for dx in range(2):
            greet(cuts=2 * chip_at(dy, dx) + core, idx=iid ^ 1)

    to_dc = selection(256, 256, lambda r, c: ((r >> 5) == (c & 7)) & ((r & 31) == (c >> 3)))
    from_dc = selection(256, 256, lambda r, c: ((c >> 5) == (r & 7)) & ((c & 31) == (r >> 3)))
    row_kc = selection(256, 256, lambda r, c: ((r >> 6) == (c >> 6)) & (((r >> 5) & 1) == (c & 1))
                       & ((r & 31) == ((c >> 1) & 31)))
    to_xlkz = selection(512, 512, lambda r, c: ((r & 1) == (c >> 8)) & (((r >> 1) & 15) == (c & 15))
                        & (((r >> 5) & 1) == ((c >> 4) & 1)) & ((r >> 6) == ((c >> 5) & 7)))

    pl.semaphore_wait(barrier, 42)

    def quarter(c):
        return pl.ds(pl.multiple_of((c >> 2) * 128, 128), 128)

    for dy, dx, dc in CUT_STEPS:
        to = 2 * chip_at(dy, dx) + (core ^ dc)
        push(COT, cot_ref.at[:, :, quarter(to)], cotr.at[cid], cuts=to)
    cotr[cid] = cot_ref[:, :, quarter(cid)]

    w1 = [dot(ws_ref[0, p], from_dc).astype(BF) for p in range(2)]
    for p in range(2):
        for h in range(2):
            rows = slice(256 * h, 256 * h + 256)
            bp[p, rows] = dot(row_kc, b_ref[p, rows]).astype(BF)
    fst[0] = dot(bp[0], w1[0]) - dot(bp[1], w1[1])
    fst[1] = dot(bp[1], w1[0]) + dot(bp[0], w1[1])
    for p in range(2):
        for d in range(8):
            for g in range(4):
                pieces = [(fst[p, 32 * (4 * g + j):32 * (4 * g + j) + 32, 128 * (d // 4):128 * (d // 4) + 128],
                           32 * (d % 4)) for j in range(4)]
                xdc[p, 32 * d:32 * d + 32, 128 * g:128 * g + 128] = join_lanes(pieces).astype(BF)
        xp[p] = dot(xdc[p], to_xlkz).astype(BF)

    for p in range(2):
        w3p[p] = dot(to_dc, w3_ref[p]).astype(BF)
    t_re = dot(w3p[0], xp[0], (0, 0)) - dot(w3p[1], xp[1], (0, 0))
    t_im = dot(w3p[0], xp[1], (0, 0)) + dot(w3p[1], xp[0], (0, 0))
    for c in range(CUTS):
        for x in range(2):
            rows, lanes = slice(16 * c, 16 * c + 16), slice(256 * x, 256 * x + 256)
            tbuf[c & 1, 8 * x + (c >> 1), 0] = t_re[rows, lanes].astype(BF)
            tbuf[c & 1, 8 * x + (c >> 1), 1] = t_im[rows, lanes].astype(BF)
    push(RS1, tbuf.at[1 - core], trecv, cuts=cid ^ 1)
    for p in range(2):
        xnat[p] = dot(from_dc, xp[p]).astype(BF)
    arrived(RS1)
    sbuf[...] = (tbuf[core].astype(F32) + trecv[...].astype(F32)).astype(BF)
    for dy, dx, flip in PLANE_STEPS:
        to, to_x = chip_at(dy, dx), xl ^ flip
        push(RS2, sbuf.at[8 * to_x + to], recv2.at[8 * xl + chip], cuts=2 * to + core, idx=2 * z + to_x)
    recv2[8 * xl + chip] = sbuf[8 * xl + chip]

    arrived(COT)
    lane0 = (cid & 3) * 32
    s_re = selection(128, 128, lambda r, c: (c < 32) & (r == c + lane0))
    s_im = selection(128, 128, lambda r, c: (c >= 32) & (c < 64) & (r == c - 32 + lane0))
    g_re = cotr[:, 0].reshape(256, 128)
    g_im = cotr[:, 1].reshape(256, 128)
    gcat[...] = (dot(g_re, s_re) + dot(g_im, s_im)).astype(BF)
    grot[...] = (dot(g_im, s_re) - dot(g_re, s_im)).astype(BF)
    g3b = dot(ws_ref[1, 0], gcat[...]) + dot(ws_ref[1, 1], grot[...])
    gsend[...] = g3b.astype(BF).reshape(16, 16, 128)
    for n in LINE:
        to = (z + n) & 15
        push(GEX, gsend.at[to], grecv.at[z], idx=2 * to + xl)
    grecv[z] = gsend[z]

    arrived(RS2)
    rows = []
    for x in range(2):
        part = recv2[8 * x].astype(F32)
        for g in range(1, 8):
            part = part + recv2[8 * x + g].astype(F32)
        rows.append(part.reshape(32, 256).astype(BF))
    rows.append(jnp.zeros((64, 256), BF))
    to_zkl = selection(256, 256, lambda r, c: ((r >> 4) == (c & 15)) & (((r >> 3) & 1) == ((c >> 4) & 1))
                       & ((r & 7) == (c >> 5)))
    tsend[...] = dot(to_zkl, jnp.concatenate(rows, axis=0), (1, 1)).astype(BF).reshape(16, 16, 128)
    for n in LINE:
        to = (z + n) & 15
        push(TEX, tsend.at[to], texr.at[z], idx=2 * to + xl)
    texr[z] = tsend[z]

    arrived(GEX)
    g_all = grecv[...].astype(F32).reshape(16, 2, 8, 128)
    for x in range(2):
        g_zl = g_all[:, x].reshape(128, 128).astype(BF)
        out = None
        for k in range(2):
            pick = selection(128, 128, lambda r, c: (c < 32) & (r < 64) & ((r >> 4) == (c >> 3))
                             & (((r >> 3) & 1) == k) & ((r & 7) == (c & 7)))
            place = selection(128, 256, lambda r, c: ((r & 7) == (c >> 5)) & (((c >> 4) & 1) == k)
                              & ((r >> 3) == (c & 15)))
            part = dot(dot(g_zl, pick).astype(BF), place, (0, 0))
            out = part if out is None else out + part
        gown[x] = out[:32].astype(BF).reshape(2, 16, 256)
    for dy, dx, flip in PLANE_STEPS:
        to_x = xl ^ flip
        push(AG1, gown.at[to_x], gt.at[core, 2 * chip + xl], cuts=2 * chip_at(dy, dx) + core, idx=2 * z + to_x)
    gt[core, 2 * chip + xl] = gown[xl]

    def push_cuts(phase, src, dst):
        for dy, dx, dc in CUT_STEPS:
            to = 2 * chip_at(dy, dx) + (core ^ dc)
            push(phase, src.at[to], dst.at[cid], cuts=to)
        dst[cid] = src[cid]

    def near(phase, src, dst):
        for step, flip in NEAR:
            to_z, to_x = (z + step) & 15, xl ^ flip
            push(phase, src.at[((to_z & 3) << 1) + to_x], dst.at[2 * (step + 1) + flip], idx=2 * to_z + to_x)
        dst[2] = src[cls]

    def near_back(phase, src, dst):
        for step, flip in NEAR:
            push(phase, src, dst.at[cls], idx=2 * ((z - step) & 15) + (xl ^ flip))

    def add_up(ref, count):
        out = ref[0].astype(F32)
        for n in range(1, count):
            out = out + ref[n].astype(F32)
        return out

    def push_far(phase, ref):
        for hop in (2, 1, 3):
            push(phase, ref.at[far], ref.at[far], idx=2 * (4 * ((far + hop) & 3) + (z & 3)) + xl)

    def grad_three(half, part):
        g = [jnp.concatenate([jnp.concatenate([gt[half, 2 * n, p], gt[half, 2 * n + 1, p]], axis=1)
                              for n in range(8)], axis=0) for p in range(2)]
        z_re = dot(xnat[0], g[0], (1, 1)) + dot(xnat[1], g[1], (1, 1))
        z_im = dot(xnat[0], g[1], (1, 1)) - dot(xnat[1], g[0], (1, 1))
        zs3[half, 0:4] = z_re.astype(BF).reshape(4, 64, 128)
        zs3[half, 4:8] = z_im.astype(BF).reshape(4, 64, 128)
        near(N3 + part, zs3.at[half], nr3.at[half])

    def sum_three(half, part):
        arrived(N3 + part)
        clsx[half, far] = add_up(nr3.at[half], 8).astype(BF)
        push_far(F3 + part, clsx.at[half])

    def spread_three(half, part):
        arrived(F3 + part)
        cls3[half] = add_up(clsx.at[half], 4).astype(BF)
        near_back(B3 + part, cls3.at[half], zfin.at[half])
        zfin[half, cls] = cls3[half]

    arrived(AG1)
    push(AG2, gt.at[core], gt.at[core], cuts=cid ^ 1)
    grad_three(core, 0)

    arrived(TEX)
    t_all = texr[...].astype(F32).reshape(16, 2, 8, 128)
    t_k = [t_all[:, k].reshape(128, 128).astype(BF) for k in range(2)]
    cat, rot = [], []
    for x in range(2):
        one = two = None
        for k in range(2):
            def same(r, c):
                return (c < 64) & ((r >> 5) == x) & (((c >> 3) & 1) == k) & ((r & 7) == (c & 7)) \
                    & (((r >> 3) & 1) == ((c >> 4) & 1))
            keep = selection(128, 128, lambda r, c: same(r, c) & (((r >> 4) & 1) == (c >> 5)))
            to_im = selection(128, 128, lambda r, c: same(r, c) & (((r >> 4) & 1) == 0) & (c >= 32))
            to_re = selection(128, 128, lambda r, c: same(r, c) & (((r >> 4) & 1) == 1) & (c < 32))
            a, b = dot(t_k[k], keep), dot(t_k[k], to_im - to_re)
            one, two = (a, b) if one is None else (one + a, two + b)
        cat.append(one.astype(BF))
        rot.append(two.astype(BF))
    to_u = selection(256, 256, lambda r, c: ((r >> 4) == ((c >> 3) & 15)) & (((r >> 3) & 1) == (c >> 7))
                     & ((r & 7) == (c & 7)))
    t_cat = dot(to_u, jnp.concatenate(cat, axis=0)).astype(BF)
    t_rot = dot(to_u, jnp.concatenate(rot, axis=0)).astype(BF)
    amp = dot(ws_ref[1, 0], t_cat, (0, 0)) + dot(ws_ref[1, 1], t_rot, (0, 0))
    low = pltpu.roll(amp - amp.astype(BF).astype(F32), 64, 1)
    amp = jnp.where(lax.broadcasted_iota(jnp.int32, (256, 128), 1) < 64, amp, low)
    z2s[:, :, 0:128] = amp.astype(BF).reshape(CUTS, 16, 128)
    z2s[:, :, 128:384] = dot(t_cat, gcat[...], (1, 1)).astype(BF).reshape(CUTS, 16, 256)
    z2s[:, :, 384:640] = dot(t_cat, grot[...], (1, 1)).astype(BF).reshape(CUTS, 16, 256)
    push_cuts(ZS2, z2s, z2r)

    arrived(AG2)
    gr, gi = [
        jnp.concatenate([jnp.concatenate([gt[c & 1, 2 * (c >> 1), p], gt[c & 1, 2 * (c >> 1) + 1, p]], axis=1)
                         for c in range(CUTS)], axis=0) for p in range(2)]
    nr, ni = [dot(g, to_xlkz, (1, 1)).astype(BF) for g in (gr, gi)]
    bk[0] = dot(w3p[0], nr) + dot(w3p[1], ni)
    bk[1] = dot(w3p[0], ni) - dot(w3p[1], nr)
    for p in range(2):
        for uk in range(16):
            for g in range(2):
                pieces = [(bk[p, 32 * (4 * g + j):32 * (4 * g + j) + 32, 128 * (uk // 4):128 * (uk // 4) + 128],
                           32 * (uk % 4)) for j in range(4)]
                b1p[p, 32 * uk:32 * uk + 32, 128 * g:128 * g + 128] = join_lanes(pieces).astype(BF)
    z_re = dot(bp[0], b1p[0], (0, 0)) + dot(bp[1], b1p[1], (0, 0))
    z_im = dot(bp[0], b1p[1], (0, 0)) - dot(bp[1], b1p[0], (0, 0))
    z1s[:, 0] = dot(z_re.astype(BF), to_dc).astype(BF).reshape(CUTS, 16, 256)
    z1s[:, 1] = dot(z_im.astype(BF), to_dc).astype(BF).reshape(CUTS, 16, 256)
    push_cuts(ZS1, z1s, z1r)

    grad_three(1 - core, 3)

    sum_three(core, 0)
    sum_three(1 - core, 3)

    arrived(ZS2)
    part = z2r[0].astype(F32)
    for n in range(1, CUTS):
        part = part + z2r[n].astype(F32)
    for p in range(2):
        ss[4 + 2 * p:6 + 2 * p] = part[:, 128 + 256 * p:384 + 256 * p].reshape(2, 8, 256)

    arrived(ZS1)
    ss[0:4] = add_up(z1r, CUTS).reshape(4, 8, 256)
    near(NS, ss, nrs)

    spread_three(core, 0)

    group = lax.broadcasted_iota(jnp.int32, (16, 128), 1) >> 5
    for g in range(4):
        blocks = [z2r[4 * g + j, :, 0:128].astype(F32) for j in range(4)]
        blocks = [b + pltpu.roll(b, 64, 1) for b in blocks]
        for p in range(2):
            out = None
            for j in range(4):
                shift = (32 * j - 32 * p) % 128
                moved = pltpu.roll(blocks[j], shift, 1) if shift else blocks[j]
                out = moved if out is None else jnp.where(group == j, moved, out)
            amp_ref[p, :, 128 * g:128 * g + 128] = out

    arrived(NS)
    fx[far] = add_up(nrs, 8)
    push_far(FS, fx)

    spread_three(1 - core, 3)

    arrived(FS)
    sfin[cls] = add_up(fx, 4)
    near_back(BS, sfin.at[cls], sfin)

    to_cut = selection(256, 256, lambda r, c: ((r >> 7) == ((c >> 4) & 1)) & (((r >> 4) & 7) == (c >> 5))
                       & ((r & 15) == (c & 15)))
    arrived(B3)
    arrived(B3 + 3)
    for n in range(8):
        block = jnp.concatenate([zfin[0, n], zfin[1, n]], axis=1)
        gl_ref[n // 4, 64 * (n % 4):64 * (n % 4) + 64] = dot(block, to_cut)
    arrived(BS)
    gs_ref[...] = sfin[...].reshape(64, 256)

    for phase in started:
        pltpu.make_async_copy(totals[phase], totals[phase], send_sem.at[phase]).wait()


def local(boundary, gates_shared, gates_sliced, cotangent):
    vmem = pltpu.VMEM
    scratch = [
        vmem((2, 512, 256), BF),
        vmem((2, 512, 256), F32),
        vmem((2, 256, 512), BF),
        vmem((2, 256, 512), BF),
        vmem((2, 256, 512), BF),
        vmem((2, 256, 256), BF),
        vmem((CUTS, 2, 16, 128), BF),
        vmem((256, 128), BF),
        vmem((256, 128), BF),
        vmem((16, 16, 128), BF),
        vmem((16, 16, 128), BF),
        vmem((2, 2, 16, 256), BF),
        vmem((2, 16, 2, 16, 256), BF),
        vmem((16, 2, 16, 256), BF),
        vmem((16, 2, 16, 256), BF),
        vmem((16, 2, 16, 256), BF),
        vmem((2, 16, 2, 16, 256), BF),
        vmem((16, 16, 128), BF),
        vmem((16, 16, 128), BF),
        vmem((2, 256, 512), F32),
        vmem((2, 512, 256), BF),
        vmem((CUTS, 2, 16, 256), BF),
        vmem((CUTS, 2, 16, 256), BF),
        vmem((CUTS, 16, 640), BF),
        vmem((CUTS, 16, 640), BF),
        vmem((2, 8, 64, 128), BF),
        vmem((2, 8, 64, 128), BF),
        vmem((2, 4, 64, 128), BF),
        vmem((2, 64, 128), BF),
        vmem((2, 8, 64, 128), BF),
        vmem((8, 8, 256), F32),
        vmem((8, 8, 256), F32),
        vmem((4, 8, 256), F32),
        vmem((8, 8, 256), F32),
        pltpu.SemaphoreType.DMA((PHASES,)),
        pltpu.SemaphoreType.DMA((PHASES,)),
    ]
    amp, shared, sliced = pl.pallas_call(
        kernel,
        out_shape=(
            jax.ShapeDtypeStruct((2, 16, 512), F32),
            jax.ShapeDtypeStruct((64, 256), F32),
            jax.ShapeDtypeStruct((2, 256, 256), F32),
        ),
        in_specs=[pl.BlockSpec(memory_space=vmem)] * 4,
        out_specs=[pl.BlockSpec(memory_space=vmem)] * 3,
        scratch_shapes=scratch,
        compiler_params=pltpu.CompilerParams(
            collective_id=0, has_side_effects=True, vmem_limit_bytes=40 * 2 ** 20),
    )(boundary.reshape(2, 512, 256), gates_shared, gates_sliced[:, 0], cotangent[:, 0])
    return amp[:, None], shared.reshape(2, 2, 16, 256), sliced[:, None]


def solution(mesh):
    return jax.shard_map(
        local,
        mesh=mesh,
        in_specs=(
            P(None, "cuts", "idx"),
            P(),
            P(None, "cuts", None, None),
            P(None, "idx", "cuts", None),
        ),
        out_specs=(
            P(None, "idx", "cuts", None),
            P(None, None, "cuts", None),
            P(None, "cuts", None, None),
        ),
        check_vma=False,
    )
```

```python
import jax
import jax.numpy as jnp
from jax import lax
from jax.experimental import pallas as pl
from jax.experimental.pallas import tpu as pltpu
from jax.sharding import PartitionSpec as P


BF = jnp.bfloat16
F32 = jnp.float32
MESH = pl.DeviceIdType.MESH
CUTS = 16

(COT, GEX, RS1, RS2, AG1, AG2, TEX, ZS2, ZS1, NS, FS, BS, N3, F3, B3) = range(15)
PHASES = 18

LINE = sorted(range(1, 16), key=lambda n: -min(n, 16 - n))
NEAR = [(2, 1), (2, 0), (-1, 1), (1, 1), (-1, 0), (1, 0), (0, 1)]


def hops(dy, dx, dc, flip):
    return min(dy, 4 - dy) + (2 if dx > flip else max(dx, flip)) + 0.5 * dc


CUT_STEPS = sorted(((dy, dx, dc) for dy in range(4) for dx in range(2) for dc in range(2) if dy + dx + dc),
                   key=lambda t: -hops(*t, 0))
PLANE_STEPS = sorted(((dy, dx, flip) for dy in range(4) for dx in range(2) for flip in range(2) if dy + dx + flip),
                     key=lambda t: -hops(t[0], t[1], 0, t[2]))


def dot(a, b, contract=(1, 0)):
    return lax.dot_general(a, b, (((contract[0],), (contract[1],)), ((), ())), preferred_element_type=F32)


def selection(rows, cols, test):
    r = lax.broadcasted_iota(jnp.int32, (rows, cols), 0)
    c = lax.broadcasted_iota(jnp.int32, (rows, cols), 1)
    return jnp.where(test(r, c), 1.0, 0.0).astype(BF)


def join_lanes(pieces):
    group = lax.broadcasted_iota(jnp.int32, (32, 128), 1) >> 5
    out = None
    for j, (block, off) in enumerate(pieces):
        shift = (32 * j - off) % 128
        moved = pltpu.roll(block, shift, 1) if shift else block
        out = moved if out is None else jnp.where(group == j, moved, out)
    return out


def kernel(b_ref, ws_ref, w3_ref, cot_ref, amp_ref, gs_ref, zfin,
           bp, fst, xdc, xp, xnat, w3p, cotr, gcat, grot, gsend, grecv, gown,
           tbuf, trecv, sbuf, recv2, gt, tsend, texr, bk, b1p,
           z1s, z1r, z2s, z2r, zs3, nr3, clsx, cls3,
           ss, nrs, fx, sfin, send_sem, recv_sem):
    cid = lax.axis_index("cuts")
    iid = lax.axis_index("idx")
    y, xh, core, chip = cid >> 2, (cid >> 1) & 1, cid & 1, cid >> 1
    z, xl = iid >> 1, iid & 1
    cls = ((z & 3) << 1) + xl
    far = z >> 2

    totals = {
        COT: cotr.at[pl.ds(0, 15)], GEX: grecv.at[pl.ds(0, 15)], RS1: trecv, RS2: recv2.at[pl.ds(0, 15)],
        AG1: gt.at[0, pl.ds(0, 15)], AG2: gt.at[0], TEX: texr.at[pl.ds(0, 15)],
        ZS2: z2r.at[pl.ds(0, 15)], ZS1: z1r.at[pl.ds(0, 15)], NS: nrs.at[pl.ds(0, 7)], FS: fx.at[pl.ds(0, 3)], BS: sfin.at[pl.ds(0, 7)]}
    for part in (0, 3):
        totals[N3 + part] = nr3.at[0, pl.ds(0, 7)]
        totals[F3 + part] = clsx.at[0, pl.ds(0, 3)]
        totals[B3 + part] = zfin.at[0, pl.ds(0, 7)]
    started = []

    def push(phase, src, dst, cuts=None, idx=None):
        if phase not in started:
            started.append(phase)
        device = {}
        if cuts is not None:
            device["cuts"] = cuts
        if idx is not None:
            device["idx"] = idx
        pltpu.make_async_remote_copy(
            src_ref=src, dst_ref=dst, send_sem=send_sem.at[phase], recv_sem=recv_sem.at[phase],
            device_id=device, device_id_type=MESH).start()

    def arrived(phase):
        pltpu.make_async_copy(totals[phase], totals[phase], recv_sem.at[phase]).wait()

    def chip_at(dy, dx):
        return (((y + dy) & 3) << 1) + (xh ^ dx)

    barrier = pltpu.get_barrier_semaphore()

    def greet(**device):
        pl.semaphore_signal(barrier, inc=1, device_id=device, device_id_type=MESH)
    for n in LINE:
        greet(idx=2 * ((z + n) & 15) + xl)
    for n in (2, 14, 1, 15):
        greet(idx=2 * ((z + n) & 15) + (xl ^ 1))
    for dy, dx, dc in CUT_STEPS:
        greet(cuts=2 * chip_at(dy, dx) + (core ^ dc))
    for dy in range(4):
        for dx in range(2):
            greet(cuts=2 * chip_at(dy, dx) + core, idx=iid ^ 1)

    to_dc = selection(256, 256, lambda r, c: ((r >> 5) == (c & 7)) & ((r & 31) == (c >> 3)))
    from_dc = selection(256, 256, lambda r, c: ((c >> 5) == (r & 7)) & ((c & 31) == (r >> 3)))
    row_kc = selection(256, 256, lambda r, c: ((r >> 6) == (c >> 6)) & (((r >> 5) & 1) == (c & 1))
                       & ((r & 31) == ((c >> 1) & 31)))
    to_xlkz = selection(512, 512, lambda r, c: ((r & 1) == (c >> 8)) & (((r >> 1) & 15) == (c & 15))
                        & (((r >> 5) & 1) == ((c >> 4) & 1)) & ((r >> 6) == ((c >> 5) & 7)))

    pl.semaphore_wait(barrier, 42)

    def quarter(c):
        return pl.ds(pl.multiple_of((c >> 2) * 128, 128), 128)

    for dy, dx, dc in CUT_STEPS:
        to = 2 * chip_at(dy, dx) + (core ^ dc)
        push(COT, cot_ref.at[:, :, quarter(to)], cotr.at[cid], cuts=to)
    cotr[cid] = cot_ref[:, :, quarter(cid)]

    w1 = [dot(ws_ref[0, p], from_dc).astype(BF) for p in range(2)]
    for p in range(2):
        for h in range(2):
            rows = slice(256 * h, 256 * h + 256)
            bp[p, rows] = dot(row_kc, b_ref[p, rows]).astype(BF)
    fst[0] = dot(bp[0], w1[0]) - dot(bp[1], w1[1])
    fst[1] = dot(bp[1], w1[0]) + dot(bp[0], w1[1])
    for p in range(2):
        for d in range(8):
            for g in range(4):
                pieces = [(fst[p, 32 * (4 * g + j):32 * (4 * g + j) + 32, 128 * (d // 4):128 * (d // 4) + 128],
                           32 * (d % 4)) for j in range(4)]
                xdc[p, 32 * d:32 * d + 32, 128 * g:128 * g + 128] = join_lanes(pieces).astype(BF)
        xp[p] = dot(xdc[p], to_xlkz).astype(BF)

    for p in range(2):
        w3p[p] = dot(to_dc, w3_ref[p]).astype(BF)
    t_re = dot(w3p[0], xp[0], (0, 0)) - dot(w3p[1], xp[1], (0, 0))
    t_im = dot(w3p[0], xp[1], (0, 0)) + dot(w3p[1], xp[0], (0, 0))
    for c in range(CUTS):
        for x in range(2):
            rows, lanes = slice(16 * c, 16 * c + 16), slice(256 * x, 256 * x + 256)
            tbuf[c & 1, 8 * x + (c >> 1), 0] = t_re[rows, lanes].astype(BF)
            tbuf[c & 1, 8 * x + (c >> 1), 1] = t_im[rows, lanes].astype(BF)
    push(RS1, tbuf.at[1 - core], trecv, cuts=cid ^ 1)
    for p in range(2):
        xnat[p] = dot(from_dc, xp[p]).astype(BF)
    arrived(RS1)
    sbuf[...] = (tbuf[core].astype(F32) + trecv[...].astype(F32)).astype(BF)
    for dy, dx, flip in PLANE_STEPS:
        to, to_x = chip_at(dy, dx), xl ^ flip
        push(RS2, sbuf.at[8 * to_x + to], recv2.at[8 * xl + chip], cuts=2 * to + core, idx=2 * z + to_x)
    recv2[8 * xl + chip] = sbuf[8 * xl + chip]

    arrived(COT)
    lane0 = (cid & 3) * 32
    s_re = selection(128, 128, lambda r, c: (c < 32) & (r == c + lane0))
    s_im = selection(128, 128, lambda r, c: (c >= 32) & (c < 64) & (r == c - 32 + lane0))
    g_re = cotr[:, 0].reshape(256, 128)
    g_im = cotr[:, 1].reshape(256, 128)
    gcat[...] = (dot(g_re, s_re) + dot(g_im, s_im)).astype(BF)
    grot[...] = (dot(g_im, s_re) - dot(g_re, s_im)).astype(BF)
    g3b = dot(ws_ref[1, 0], gcat[...]) + dot(ws_ref[1, 1], grot[...])
    gsend[...] = g3b.astype(BF).reshape(16, 16, 128)
    for n in LINE:
        to = (z + n) & 15
        push(GEX, gsend.at[to], grecv.at[z], idx=2 * to + xl)
    grecv[z] = gsend[z]

    arrived(RS2)
    rows = []
    for x in range(2):
        part = recv2[8 * x].astype(F32)
        for g in range(1, 8):
            part = part + recv2[8 * x + g].astype(F32)
        rows.append(part.reshape(32, 256).astype(BF))
    rows.append(jnp.zeros((64, 256), BF))
    to_zkl = selection(256, 256, lambda r, c: ((r >> 4) == (c & 15)) & (((r >> 3) & 1) == ((c >> 4) & 1))
                       & ((r & 7) == (c >> 5)))
    tsend[...] = dot(to_zkl, jnp.concatenate(rows, axis=0), (1, 1)).astype(BF).reshape(16, 16, 128)
    for n in LINE:
        to = (z + n) & 15
        push(TEX, tsend.at[to], texr.at[z], idx=2 * to + xl)
    texr[z] = tsend[z]

    arrived(GEX)
    g_all = grecv[...].astype(F32).reshape(16, 2, 8, 128)
    for x in range(2):
        g_zl = g_all[:, x].reshape(128, 128).astype(BF)
        out = None
        for k in range(2):
            pick = selection(128, 128, lambda r, c: (c < 32) & (r < 64) & ((r >> 4) == (c >> 3))
                             & (((r >> 3) & 1) == k) & ((r & 7) == (c & 7)))
            place = selection(128, 256, lambda r, c: ((r & 7) == (c >> 5)) & (((c >> 4) & 1) == k)
                              & ((r >> 3) == (c & 15)))
            part = dot(dot(g_zl, pick).astype(BF), place, (0, 0))
            out = part if out is None else out + part
        gown[x] = out[:32].astype(BF).reshape(2, 16, 256)
    for dy, dx, flip in PLANE_STEPS:
        to_x = xl ^ flip
        push(AG1, gown.at[to_x], gt.at[core, 2 * chip + xl], cuts=2 * chip_at(dy, dx) + core, idx=2 * z + to_x)
    gt[core, 2 * chip + xl] = gown[xl]

    def push_cuts(phase, src, dst):
        for dy, dx, dc in CUT_STEPS:
            to = 2 * chip_at(dy, dx) + (core ^ dc)
            push(phase, src.at[to], dst.at[cid], cuts=to)
        dst[cid] = src[cid]

    def near(phase, src, dst):
        for step, flip in NEAR:
            to_z, to_x = (z + step) & 15, xl ^ flip
            push(phase, src.at[((to_z & 3) << 1) + to_x], dst.at[2 * (step + 1) + flip], idx=2 * to_z + to_x)
        dst[2] = src[cls]

    def near_back(phase, src, dst):
        for step, flip in NEAR:
            push(phase, src, dst.at[cls], idx=2 * ((z - step) & 15) + (xl ^ flip))

    def add_up(ref, count):
        out = ref[0].astype(F32)
        for n in range(1, count):
            out = out + ref[n].astype(F32)
        return out

    def push_far(phase, ref):
        for hop in (2, 1, 3):
            push(phase, ref.at[far], ref.at[far], idx=2 * (4 * ((far + hop) & 3) + (z & 3)) + xl)

    def grad_three(half, part):
        g = [jnp.concatenate([jnp.concatenate([gt[half, 2 * n, p], gt[half, 2 * n + 1, p]], axis=1)
                              for n in range(8)], axis=0) for p in range(2)]
        z_re = dot(xnat[0], g[0], (1, 1)) + dot(xnat[1], g[1], (1, 1))
        z_im = dot(xnat[0], g[1], (1, 1)) - dot(xnat[1], g[0], (1, 1))
        zs3[half, 0:4] = z_re.astype(BF).reshape(4, 64, 128)
        zs3[half, 4:8] = z_im.astype(BF).reshape(4, 64, 128)
        near(N3 + part, zs3.at[half], nr3.at[half])

    def sum_three(half, part):
        arrived(N3 + part)
        clsx[half, far] = add_up(nr3.at[half], 8).astype(BF)
        push_far(F3 + part, clsx.at[half])

    def spread_three(half, part):
        arrived(F3 + part)
        cls3[half] = add_up(clsx.at[half], 4).astype(BF)
        near_back(B3 + part, cls3.at[half], zfin.at[half])
        zfin[half, cls] = cls3[half]

    arrived(AG1)
    push(AG2, gt.at[core], gt.at[core], cuts=cid ^ 1)
    grad_three(core, 0)

    arrived(TEX)
    t_all = texr[...].astype(F32).reshape(16, 2, 8, 128)
    t_k = [t_all[:, k].reshape(128, 128).astype(BF) for k in range(2)]
    cat, rot = [], []
    for x in range(2):
        one = two = None
        for k in range(2):
            def same(r, c):
                return (c < 64) & ((r >> 5) == x) & (((c >> 3) & 1) == k) & ((r & 7) == (c & 7)) \
                    & (((r >> 3) & 1) == ((c >> 4) & 1))
            keep = selection(128, 128, lambda r, c: same(r, c) & (((r >> 4) & 1) == (c >> 5)))
            to_im = selection(128, 128, lambda r, c: same(r, c) & (((r >> 4) & 1) == 0) & (c >= 32))
            to_re = selection(128, 128, lambda r, c: same(r, c) & (((r >> 4) & 1) == 1) & (c < 32))
            a, b = dot(t_k[k], keep), dot(t_k[k], to_im - to_re)
            one, two = (a, b) if one is None else (one + a, two + b)
        cat.append(one.astype(BF))
        rot.append(two.astype(BF))
    to_u = selection(256, 256, lambda r, c: ((r >> 4) == ((c >> 3) & 15)) & (((r >> 3) & 1) == (c >> 7))
                     & ((r & 7) == (c & 7)))
    t_cat = dot(to_u, jnp.concatenate(cat, axis=0)).astype(BF)
    t_rot = dot(to_u, jnp.concatenate(rot, axis=0)).astype(BF)
    amp = dot(ws_ref[1, 0], t_cat, (0, 0)) + dot(ws_ref[1, 1], t_rot, (0, 0))
    low = pltpu.roll(amp - amp.astype(BF).astype(F32), 64, 1)
    amp = jnp.where(lax.broadcasted_iota(jnp.int32, (256, 128), 1) < 64, amp, low)
    z2s[:, :, 0:128] = amp.astype(BF).reshape(CUTS, 16, 128)
    z2s[:, :, 128:384] = dot(t_cat, gcat[...], (1, 1)).astype(BF).reshape(CUTS, 16, 256)
    z2s[:, :, 384:640] = dot(t_cat, grot[...], (1, 1)).astype(BF).reshape(CUTS, 16, 256)
    push_cuts(ZS2, z2s, z2r)

    arrived(AG2)
    gr, gi = [
        jnp.concatenate([jnp.concatenate([gt[c & 1, 2 * (c >> 1), p], gt[c & 1, 2 * (c >> 1) + 1, p]], axis=1)
                         for c in range(CUTS)], axis=0) for p in range(2)]
    nr, ni = [dot(g, to_xlkz, (1, 1)).astype(BF) for g in (gr, gi)]
    bk[0] = dot(w3p[0], nr) + dot(w3p[1], ni)
    bk[1] = dot(w3p[0], ni) - dot(w3p[1], nr)
    for p in range(2):
        for uk in range(16):
            for g in range(2):
                pieces = [(bk[p, 32 * (4 * g + j):32 * (4 * g + j) + 32, 128 * (uk // 4):128 * (uk // 4) + 128],
                           32 * (uk % 4)) for j in range(4)]
                b1p[p, 32 * uk:32 * uk + 32, 128 * g:128 * g + 128] = join_lanes(pieces).astype(BF)
    z_re = dot(bp[0], b1p[0], (0, 0)) + dot(bp[1], b1p[1], (0, 0))
    z_im = dot(bp[0], b1p[1], (0, 0)) - dot(bp[1], b1p[0], (0, 0))
    z1s[:, 0] = dot(z_re.astype(BF), to_dc).astype(BF).reshape(CUTS, 16, 256)
    z1s[:, 1] = dot(z_im.astype(BF), to_dc).astype(BF).reshape(CUTS, 16, 256)
    push_cuts(ZS1, z1s, z1r)

    grad_three(1 - core, 3)

    sum_three(core, 0)
    sum_three(1 - core, 3)

    arrived(ZS2)
    part = z2r[0].astype(F32)
    for n in range(1, CUTS):
        part = part + z2r[n].astype(F32)
    for p in range(2):
        ss[4 + 2 * p:6 + 2 * p] = part[:, 128 + 256 * p:384 + 256 * p].reshape(2, 8, 256)

    arrived(ZS1)
    ss[0:4] = add_up(z1r, CUTS).reshape(4, 8, 256)
    near(NS, ss, nrs)

    group = lax.broadcasted_iota(jnp.int32, (16, 128), 1) >> 5
    for g in range(4):
        blocks = [z2r[4 * g + j, :, 0:128].astype(F32) for j in range(4)]
        blocks = [b + pltpu.roll(b, 64, 1) for b in blocks]
        for p in range(2):
            out = None
            for j in range(4):
                shift = (32 * j - 32 * p) % 128
                moved = pltpu.roll(blocks[j], shift, 1) if shift else blocks[j]
                out = moved if out is None else jnp.where(group == j, moved, out)
            amp_ref[p, :, 128 * g:128 * g + 128] = out

    arrived(NS)
    fx[far] = add_up(nrs, 8)
    push_far(FS, fx)

    spread_three(core, 0)
    spread_three(1 - core, 3)

    arrived(FS)
    sfin[cls] = add_up(fx, 4)
    near_back(BS, sfin.at[cls], sfin)

    arrived(B3)
    arrived(B3 + 3)
    arrived(BS)
    gs_ref[...] = sfin[...].reshape(64, 256)

    for phase in started:
        pltpu.make_async_copy(totals[phase], totals[phase], send_sem.at[phase]).wait()


def results(amp_ref, gs_ref, zfin, amp_hbm, gs_hbm, gl_hbm, stage, sem):
    stores = [pltpu.make_async_copy(amp_ref, amp_hbm, sem.at[0]), pltpu.make_async_copy(gs_ref, gs_hbm, sem.at[1])]
    for store in stores:
        store.start()
    to_cut = selection(256, 256, lambda r, c: ((r >> 7) == ((c >> 4) & 1)) & (((r >> 4) & 7) == (c >> 5))
                       & ((r & 15) == (c & 15)))
    for p in range(2):
        for n in range(4):
            block = jnp.concatenate([zfin[0, 4 * p + n], zfin[1, 4 * p + n]], axis=1)
            stage[p, 64 * n:64 * n + 64] = dot(block, to_cut)
        stores.append(pltpu.make_async_copy(stage.at[p], gl_hbm.at[p], sem.at[2 + p]))
        stores[-1].start()
    for store in stores:
        store.wait()


def local(boundary, gates_shared, gates_sliced, cotangent):
    vmem = pltpu.VMEM
    scratch = [
        vmem((2, 512, 256), BF),
        vmem((2, 512, 256), F32),
        vmem((2, 256, 512), BF),
        vmem((2, 256, 512), BF),
        vmem((2, 256, 512), BF),
        vmem((2, 256, 256), BF),
        vmem((CUTS, 2, 16, 128), BF),
        vmem((256, 128), BF),
        vmem((256, 128), BF),
        vmem((16, 16, 128), BF),
        vmem((16, 16, 128), BF),
        vmem((2, 2, 16, 256), BF),
        vmem((2, 16, 2, 16, 256), BF),
        vmem((16, 2, 16, 256), BF),
        vmem((16, 2, 16, 256), BF),
        vmem((16, 2, 16, 256), BF),
        vmem((2, 16, 2, 16, 256), BF),
        vmem((16, 16, 128), BF),
        vmem((16, 16, 128), BF),
        vmem((2, 256, 512), F32),
        vmem((2, 512, 256), BF),
        vmem((CUTS, 2, 16, 256), BF),
        vmem((CUTS, 2, 16, 256), BF),
        vmem((CUTS, 16, 640), BF),
        vmem((CUTS, 16, 640), BF),
        vmem((2, 8, 64, 128), BF),
        vmem((2, 8, 64, 128), BF),
        vmem((2, 4, 64, 128), BF),
        vmem((2, 64, 128), BF),
        vmem((8, 8, 256), F32),
        vmem((8, 8, 256), F32),
        vmem((4, 8, 256), F32),
        vmem((8, 8, 256), F32),
        pltpu.SemaphoreType.DMA((PHASES,)),
        pltpu.SemaphoreType.DMA((PHASES,)),
    ]
    hbm = pl.BlockSpec(memory_space=pltpu.HBM)
    whole = pl.BlockSpec(memory_space=vmem)
    parts = pl.pallas_call(
        kernel,
        out_shape=(
            jax.ShapeDtypeStruct((2, 16, 512), F32),
            jax.ShapeDtypeStruct((64, 256), F32),
            jax.ShapeDtypeStruct((2, 8, 64, 128), BF),
        ),
        in_specs=[whole] * 4,
        out_specs=[whole] * 3,
        scratch_shapes=scratch,
        compiler_params=pltpu.CompilerParams(
            collective_id=0, has_side_effects=True, vmem_limit_bytes=40 * 2 ** 20),
    )(boundary.reshape(2, 512, 256), gates_shared, gates_sliced[:, 0], cotangent[:, 0])
    amp, shared, sliced = pl.pallas_call(
        results,
        out_shape=(
            jax.ShapeDtypeStruct((2, 16, 512), F32),
            jax.ShapeDtypeStruct((64, 256), F32),
            jax.ShapeDtypeStruct((2, 256, 256), F32),
        ),
        in_specs=[whole] * 3,
        out_specs=[hbm] * 3,
        scratch_shapes=[vmem((2, 256, 256), F32), pltpu.SemaphoreType.DMA((4,))],
        compiler_params=pltpu.CompilerParams(vmem_limit_bytes=8 * 2 ** 20),
    )(*parts)
    return amp[:, None], shared.reshape(2, 2, 16, 256), sliced[:, None]


def solution(mesh):
    return jax.shard_map(
        local,
        mesh=mesh,
        in_specs=(
            P(None, "cuts", "idx"),
            P(),
            P(None, "cuts", None, None),
            P(None, "idx", "cuts", None),
        ),
        out_specs=(
            P(None, "idx", "cuts", None),
            P(None, None, "cuts", None),
            P(None, "cuts", None, None),
        ),
        check_vma=False,
    )
```

```python
import jax
import jax.numpy as jnp
from jax import lax
from jax.experimental import pallas as pl
from jax.experimental.pallas import tpu as pltpu
from jax.sharding import PartitionSpec as P


BF = jnp.bfloat16
F32 = jnp.float32
MESH = pl.DeviceIdType.MESH
CUTS = 16

(COT, GEX, RS1, RS2, AG1, AG2, TEX, ZS2, ZS1, NS, FS, BS, N3, F3, B3) = range(15)
PHASES = 18

LINE = sorted(range(1, 16), key=lambda n: -min(n, 16 - n))
NEAR = [(2, 1), (2, 0), (-1, 1), (1, 1), (-1, 0), (1, 0), (0, 1)]


def hops(dy, dx, dc, flip):
    return min(dy, 4 - dy) + (2 if dx > flip else max(dx, flip)) + 0.5 * dc


CUT_STEPS = sorted(((dy, dx, dc) for dy in range(4) for dx in range(2) for dc in range(2) if dy + dx + dc),
                   key=lambda t: -hops(*t, 0))
PLANE_STEPS = sorted(((dy, dx, flip) for dy in range(4) for dx in range(2) for flip in range(2) if dy + dx + flip),
                     key=lambda t: -hops(t[0], t[1], 0, t[2]))


def dot(a, b, contract=(1, 0)):
    return lax.dot_general(a, b, (((contract[0],), (contract[1],)), ((), ())), preferred_element_type=F32)


def selection(rows, cols, test):
    r = lax.broadcasted_iota(jnp.int32, (rows, cols), 0)
    c = lax.broadcasted_iota(jnp.int32, (rows, cols), 1)
    return jnp.where(test(r, c), 1.0, 0.0).astype(BF)


def join_lanes(pieces):
    group = lax.broadcasted_iota(jnp.int32, (32, 128), 1) >> 5
    out = None
    for j, (block, off) in enumerate(pieces):
        shift = (32 * j - off) % 128
        moved = pltpu.roll(block, shift, 1) if shift else block
        out = moved if out is None else jnp.where(group == j, moved, out)
    return out


def kernel(b_ref, ws_ref, w3_ref, cot_ref, amp_ref, gs_ref, gl_ref,
           bp, fst, xdc, xp, xnat, w3p, cotr, gcat, grot, gsend, grecv, gown,
           tbuf, trecv, sbuf, recv2, gt, tsend, texr, bk, b1p,
           z1s, z1r, z2s, z2r, zs3, nr3, clsx, cls3, zfin,
           ss, nrs, fx, sfin, send_sem, recv_sem):
    cid = lax.axis_index("cuts")
    iid = lax.axis_index("idx")
    y, xh, core, chip = cid >> 2, (cid >> 1) & 1, cid & 1, cid >> 1
    z, xl = iid >> 1, iid & 1
    cls = ((z & 3) << 1) + xl
    far = z >> 2

    totals = {
        COT: cotr.at[pl.ds(0, 15)], GEX: grecv.at[pl.ds(0, 15)], RS1: trecv, RS2: recv2.at[pl.ds(0, 15)],
        AG1: gt.at[0, pl.ds(0, 15)], AG2: gt.at[0], TEX: texr.at[pl.ds(0, 15)],
        ZS2: z2r.at[pl.ds(0, 15)], ZS1: z1r.at[pl.ds(0, 15)], NS: nrs.at[pl.ds(0, 7)], FS: fx.at[pl.ds(0, 3)], BS: sfin.at[pl.ds(0, 7)]}
    for part in (0, 3):
        totals[N3 + part] = nr3.at[0, pl.ds(0, 7)]
        totals[F3 + part] = clsx.at[0, pl.ds(0, 3)]
        totals[B3 + part] = zfin.at[0, pl.ds(0, 7)]
    started = []

    def push(phase, src, dst, cuts=None, idx=None):
        if phase not in started:
            started.append(phase)
        device = {}
        if cuts is not None:
            device["cuts"] = cuts
        if idx is not None:
            device["idx"] = idx
        pltpu.make_async_remote_copy(
            src_ref=src, dst_ref=dst, send_sem=send_sem.at[phase], recv_sem=recv_sem.at[phase],
            device_id=device, device_id_type=MESH).start()

    def arrived(phase):
        pltpu.make_async_copy(totals[phase], totals[phase], recv_sem.at[phase]).wait()

    def chip_at(dy, dx):
        return (((y + dy) & 3) << 1) + (xh ^ dx)

    barrier = pltpu.get_barrier_semaphore()

    def greet(**device):
        pl.semaphore_signal(barrier, inc=1, device_id=device, device_id_type=MESH)
    for n in LINE:
        greet(idx=2 * ((z + n) & 15) + xl)
    for n in (2, 14, 1, 15):
        greet(idx=2 * ((z + n) & 15) + (xl ^ 1))
    for dy, dx, dc in CUT_STEPS:
        greet(cuts=2 * chip_at(dy, dx) + (core ^ dc))
    for dy in range(4):
        for dx in range(2):
            greet(cuts=2 * chip_at(dy, dx) + core, idx=iid ^ 1)

    to_dc = selection(256, 256, lambda r, c: ((r >> 5) == (c & 7)) & ((r & 31) == (c >> 3)))
    from_dc = selection(256, 256, lambda r, c: ((c >> 5) == (r & 7)) & ((c & 31) == (r >> 3)))
    row_kc = selection(256, 256, lambda r, c: ((r >> 6) == (c >> 6)) & (((r >> 5) & 1) == (c & 1))
                       & ((r & 31) == ((c >> 1) & 31)))
    to_xlkz = selection(512, 512, lambda r, c: ((r & 1) == (c >> 8)) & (((r >> 1) & 15) == (c & 15))
                        & (((r >> 5) & 1) == ((c >> 4) & 1)) & ((r >> 6) == ((c >> 5) & 7)))

    pl.semaphore_wait(barrier, 42)

    def quarter(c):
        return pl.ds(pl.multiple_of((c >> 2) * 128, 128), 128)

    for dy, dx, dc in CUT_STEPS:
        to = 2 * chip_at(dy, dx) + (core ^ dc)
        push(COT, cot_ref.at[:, :, quarter(to)], cotr.at[cid], cuts=to)
    cotr[cid] = cot_ref[:, :, quarter(cid)]

    w1 = [dot(ws_ref[0, p], from_dc).astype(BF) for p in range(2)]
    for p in range(2):
        for h in range(2):
            rows = slice(256 * h, 256 * h + 256)
            bp[p, rows] = dot(row_kc, b_ref[p, rows]).astype(BF)
    fst[0] = dot(bp[0], w1[0]) - dot(bp[1], w1[1])
    fst[1] = dot(bp[1], w1[0]) + dot(bp[0], w1[1])
    for p in range(2):
        for d in range(8):
            for g in range(4):
                pieces = [(fst[p, 32 * (4 * g + j):32 * (4 * g + j) + 32, 128 * (d // 4):128 * (d // 4) + 128],
                           32 * (d % 4)) for j in range(4)]
                xdc[p, 32 * d:32 * d + 32, 128 * g:128 * g + 128] = join_lanes(pieces).astype(BF)
        xp[p] = dot(xdc[p], to_xlkz).astype(BF)

    for p in range(2):
        w3p[p] = dot(to_dc, w3_ref[p]).astype(BF)
    t_re = dot(w3p[0], xp[0], (0, 0)) - dot(w3p[1], xp[1], (0, 0))
    t_im = dot(w3p[0], xp[1], (0, 0)) + dot(w3p[1], xp[0], (0, 0))
    for c in range(CUTS):
        for x in range(2):
            rows, lanes = slice(16 * c, 16 * c + 16), slice(256 * x, 256 * x + 256)
            tbuf[c & 1, 8 * x + (c >> 1), 0] = t_re[rows, lanes].astype(BF)
            tbuf[c & 1, 8 * x + (c >> 1), 1] = t_im[rows, lanes].astype(BF)
    push(RS1, tbuf.at[1 - core], trecv, cuts=cid ^ 1)
    for p in range(2):
        xnat[p] = dot(from_dc, xp[p]).astype(BF)
    arrived(RS1)
    sbuf[...] = (tbuf[core].astype(F32) + trecv[...].astype(F32)).astype(BF)
    for dy, dx, flip in PLANE_STEPS:
        to, to_x = chip_at(dy, dx), xl ^ flip
        push(RS2, sbuf.at[8 * to_x + to], recv2.at[8 * xl + chip], cuts=2 * to + core, idx=2 * z + to_x)
    recv2[8 * xl + chip] = sbuf[8 * xl + chip]

    arrived(COT)
    lane0 = (cid & 3) * 32
    s_re = selection(128, 128, lambda r, c: (c < 32) & (r == c + lane0))
    s_im = selection(128, 128, lambda r, c: (c >= 32) & (c < 64) & (r == c - 32 + lane0))
    g_re = cotr[:, 0].reshape(256, 128)
    g_im = cotr[:, 1].reshape(256, 128)
    gcat[...] = (dot(g_re, s_re) + dot(g_im, s_im)).astype(BF)
    grot[...] = (dot(g_im, s_re) - dot(g_re, s_im)).astype(BF)
    g3b = dot(ws_ref[1, 0], gcat[...]) + dot(ws_ref[1, 1], grot[...])
    gsend[...] = g3b.astype(BF).reshape(16, 16, 128)
    for n in LINE:
        to = (z + n) & 15
        push(GEX, gsend.at[to], grecv.at[z], idx=2 * to + xl)
    grecv[z] = gsend[z]

    arrived(RS2)
    rows = []
    for x in range(2):
        part = recv2[8 * x].astype(F32)
        for g in range(1, 8):
            part = part + recv2[8 * x + g].astype(F32)
        rows.append(part.reshape(32, 256).astype(BF))
    rows.append(jnp.zeros((64, 256), BF))
    to_zkl = selection(256, 256, lambda r, c: ((r >> 4) == (c & 15)) & (((r >> 3) & 1) == ((c >> 4) & 1))
                       & ((r & 7) == (c >> 5)))
    tsend[...] = dot(to_zkl, jnp.concatenate(rows, axis=0), (1, 1)).astype(BF).reshape(16, 16, 128)
    for n in LINE:
        to = (z + n) & 15
        push(TEX, tsend.at[to], texr.at[z], idx=2 * to + xl)
    texr[z] = tsend[z]

    arrived(GEX)
    g_all = grecv[...].astype(F32).reshape(16, 2, 8, 128)
    for x in range(2):
        g_zl = g_all[:, x].reshape(128, 128).astype(BF)
        out = None
        for k in range(2):
            pick = selection(128, 128, lambda r, c: (c < 32) & (r < 64) & ((r >> 4) == (c >> 3))
                             & (((r >> 3) & 1) == k) & ((r & 7) == (c & 7)))
            place = selection(128, 256, lambda r, c: ((r & 7) == (c >> 5)) & (((c >> 4) & 1) == k)
                              & ((r >> 3) == (c & 15)))
            part = dot(dot(g_zl, pick).astype(BF), place, (0, 0))
            out = part if out is None else out + part
        gown[x] = out[:32].astype(BF).reshape(2, 16, 256)
    for dy, dx, flip in PLANE_STEPS:
        to_x = xl ^ flip
        push(AG1, gown.at[to_x], gt.at[core, 2 * chip + xl], cuts=2 * chip_at(dy, dx) + core, idx=2 * z + to_x)
    gt[core, 2 * chip + xl] = gown[xl]

    def push_cuts(phase, src, dst):
        for dy, dx, dc in CUT_STEPS:
            to = 2 * chip_at(dy, dx) + (core ^ dc)
            push(phase, src.at[to], dst.at[cid], cuts=to)
        dst[cid] = src[cid]

    def near(phase, src, dst):
        for step, flip in NEAR:
            to_z, to_x = (z + step) & 15, xl ^ flip
            push(phase, src.at[((to_z & 3) << 1) + to_x], dst.at[2 * (step + 1) + flip], idx=2 * to_z + to_x)
        dst[2] = src[cls]

    def near_back(phase, src, dst):
        for step, flip in NEAR:
            push(phase, src, dst.at[cls], idx=2 * ((z - step) & 15) + (xl ^ flip))

    def add_up(ref, count):
        out = ref[0].astype(F32)
        for n in range(1, count):
            out = out + ref[n].astype(F32)
        return out

    def push_far(phase, ref):
        for hop in (2, 1, 3):
            push(phase, ref.at[far], ref.at[far], idx=2 * (4 * ((far + hop) & 3) + (z & 3)) + xl)

    def grad_three(half, part):
        g = [jnp.concatenate([jnp.concatenate([gt[half, 2 * n, p], gt[half, 2 * n + 1, p]], axis=1)
                              for n in range(8)], axis=0) for p in range(2)]
        z_re = dot(xnat[0], g[0], (1, 1)) + dot(xnat[1], g[1], (1, 1))
        z_im = dot(xnat[0], g[1], (1, 1)) - dot(xnat[1], g[0], (1, 1))
        zs3[half, 0:4] = z_re.astype(BF).reshape(4, 64, 128)
        zs3[half, 4:8] = z_im.astype(BF).reshape(4, 64, 128)
        near(N3 + part, zs3.at[half], nr3.at[half])

    def sum_three(half, part):
        arrived(N3 + part)
        clsx[half, far] = add_up(nr3.at[half], 8).astype(BF)
        push_far(F3 + part, clsx.at[half])

    def spread_three(half, part):
        arrived(F3 + part)
        cls3[half] = add_up(clsx.at[half], 4).astype(BF)
        near_back(B3 + part, cls3.at[half], zfin.at[half])
        zfin[half, cls] = cls3[half]

    arrived(AG1)
    push(AG2, gt.at[core], gt.at[core], cuts=cid ^ 1)
    grad_three(core, 0)

    arrived(TEX)
    t_all = texr[...].astype(F32).reshape(16, 2, 8, 128)
    t_k = [t_all[:, k].reshape(128, 128).astype(BF) for k in range(2)]
    cat, rot = [], []
    for x in range(2):
        one = two = None
        for k in range(2):
            def same(r, c):
                return (c < 64) & ((r >> 5) == x) & (((c >> 3) & 1) == k) & ((r & 7) == (c & 7)) \
                    & (((r >> 3) & 1) == ((c >> 4) & 1))
            keep = selection(128, 128, lambda r, c: same(r, c) & (((r >> 4) & 1) == (c >> 5)))
            to_im = selection(128, 128, lambda r, c: same(r, c) & (((r >> 4) & 1) == 0) & (c >= 32))
            to_re = selection(128, 128, lambda r, c: same(r, c) & (((r >> 4) & 1) == 1) & (c < 32))
            a, b = dot(t_k[k], keep), dot(t_k[k], to_im - to_re)
            one, two = (a, b) if one is None else (one + a, two + b)
        cat.append(one.astype(BF))
        rot.append(two.astype(BF))
    to_u = selection(256, 256, lambda r, c: ((r >> 4) == ((c >> 3) & 15)) & (((r >> 3) & 1) == (c >> 7))
                     & ((r & 7) == (c & 7)))
    t_cat = dot(to_u, jnp.concatenate(cat, axis=0)).astype(BF)
    t_rot = dot(to_u, jnp.concatenate(rot, axis=0)).astype(BF)
    amp = dot(ws_ref[1, 0], t_cat, (0, 0)) + dot(ws_ref[1, 1], t_rot, (0, 0))
    low = pltpu.roll(amp - amp.astype(BF).astype(F32), 64, 1)
    amp = jnp.where(lax.broadcasted_iota(jnp.int32, (256, 128), 1) < 64, amp, low)
    z2s[:, :, 0:128] = amp.astype(BF).reshape(CUTS, 16, 128)
    z2s[:, :, 128:384] = dot(t_cat, gcat[...], (1, 1)).astype(BF).reshape(CUTS, 16, 256)
    z2s[:, :, 384:640] = dot(t_cat, grot[...], (1, 1)).astype(BF).reshape(CUTS, 16, 256)
    push_cuts(ZS2, z2s, z2r)

    arrived(AG2)
    grad_three(1 - core, 3)
    gr, gi = [
        jnp.concatenate([jnp.concatenate([gt[c & 1, 2 * (c >> 1), p], gt[c & 1, 2 * (c >> 1) + 1, p]], axis=1)
                         for c in range(CUTS)], axis=0) for p in range(2)]
    nr, ni = [dot(g, to_xlkz, (1, 1)).astype(BF) for g in (gr, gi)]
    bk[0] = dot(w3p[0], nr) + dot(w3p[1], ni)
    bk[1] = dot(w3p[0], ni) - dot(w3p[1], nr)
    for p in range(2):
        for uk in range(16):
            for g in range(2):
                pieces = [(bk[p, 32 * (4 * g + j):32 * (4 * g + j) + 32, 128 * (uk // 4):128 * (uk // 4) + 128],
                           32 * (uk % 4)) for j in range(4)]
                b1p[p, 32 * uk:32 * uk + 32, 128 * g:128 * g + 128] = join_lanes(pieces).astype(BF)
    z_re = dot(bp[0], b1p[0], (0, 0)) + dot(bp[1], b1p[1], (0, 0))
    z_im = dot(bp[0], b1p[1], (0, 0)) - dot(bp[1], b1p[0], (0, 0))
    z1s[:, 0] = dot(z_re.astype(BF), to_dc).astype(BF).reshape(CUTS, 16, 256)
    z1s[:, 1] = dot(z_im.astype(BF), to_dc).astype(BF).reshape(CUTS, 16, 256)
    push_cuts(ZS1, z1s, z1r)

    sum_three(core, 0)
    sum_three(1 - core, 3)

    arrived(ZS2)
    part = z2r[0].astype(F32)
    for n in range(1, CUTS):
        part = part + z2r[n].astype(F32)
    for p in range(2):
        ss[4 + 2 * p:6 + 2 * p] = part[:, 128 + 256 * p:384 + 256 * p].reshape(2, 8, 256)

    arrived(ZS1)
    ss[0:4] = add_up(z1r, CUTS).reshape(4, 8, 256)
    near(NS, ss, nrs)

    group = lax.broadcasted_iota(jnp.int32, (16, 128), 1) >> 5
    for g in range(4):
        blocks = [z2r[4 * g + j, :, 0:128].astype(F32) for j in range(4)]
        blocks = [b + pltpu.roll(b, 64, 1) for b in blocks]
        for p in range(2):
            out = None
            for j in range(4):
                shift = (32 * j - 32 * p) % 128
                moved = pltpu.roll(blocks[j], shift, 1) if shift else blocks[j]
                out = moved if out is None else jnp.where(group == j, moved, out)
            amp_ref[p, :, 128 * g:128 * g + 128] = out

    arrived(NS)
    fx[far] = add_up(nrs, 8)
    push_far(FS, fx)

    spread_three(core, 0)
    spread_three(1 - core, 3)

    arrived(FS)
    sfin[cls] = add_up(fx, 4)
    near_back(BS, sfin.at[cls], sfin)

    arrived(B3)
    arrived(B3 + 3)
    to_cut = selection(256, 256, lambda r, c: ((r >> 7) == ((c >> 4) & 1)) & (((r >> 4) & 7) == (c >> 5))
                       & ((r & 15) == (c & 15)))
    for n in range(8):
        block = jnp.concatenate([zfin[0, n], zfin[1, n]], axis=1)
        gl_ref[n // 4, 64 * (n % 4):64 * (n % 4) + 64] = dot(block, to_cut)
    arrived(BS)
    gs_ref[...] = sfin[...].reshape(64, 256)

    for phase in started:
        pltpu.make_async_copy(totals[phase], totals[phase], send_sem.at[phase]).wait()


def results(amp_ref, gs_ref, gl_ref, amp_hbm, gs_hbm, gl_hbm, sem):
    stores = [pltpu.make_async_copy(src, dst, sem.at[n]) for n, (src, dst) in enumerate(
        ((gl_ref, gl_hbm), (amp_ref, amp_hbm), (gs_ref, gs_hbm)))]
    for store in stores:
        store.start()
    for store in stores:
        store.wait()


def local(boundary, gates_shared, gates_sliced, cotangent):
    vmem = pltpu.VMEM
    scratch = [
        vmem((2, 512, 256), BF),
        vmem((2, 512, 256), F32),
        vmem((2, 256, 512), BF),
        vmem((2, 256, 512), BF),
        vmem((2, 256, 512), BF),
        vmem((2, 256, 256), BF),
        vmem((CUTS, 2, 16, 128), BF),
        vmem((256, 128), BF),
        vmem((256, 128), BF),
        vmem((16, 16, 128), BF),
        vmem((16, 16, 128), BF),
        vmem((2, 2, 16, 256), BF),
        vmem((2, 16, 2, 16, 256), BF),
        vmem((16, 2, 16, 256), BF),
        vmem((16, 2, 16, 256), BF),
        vmem((16, 2, 16, 256), BF),
        vmem((2, 16, 2, 16, 256), BF),
        vmem((16, 16, 128), BF),
        vmem((16, 16, 128), BF),
        vmem((2, 256, 512), F32),
        vmem((2, 512, 256), BF),
        vmem((CUTS, 2, 16, 256), BF),
        vmem((CUTS, 2, 16, 256), BF),
        vmem((CUTS, 16, 640), BF),
        vmem((CUTS, 16, 640), BF),
        vmem((2, 8, 64, 128), BF),
        vmem((2, 8, 64, 128), BF),
        vmem((2, 4, 64, 128), BF),
        vmem((2, 64, 128), BF),
        vmem((2, 8, 64, 128), BF),
        vmem((8, 8, 256), F32),
        vmem((8, 8, 256), F32),
        vmem((4, 8, 256), F32),
        vmem((8, 8, 256), F32),
        pltpu.SemaphoreType.DMA((PHASES,)),
        pltpu.SemaphoreType.DMA((PHASES,)),
    ]
    hbm = pl.BlockSpec(memory_space=pltpu.HBM)
    whole = pl.BlockSpec(memory_space=vmem)
    parts = pl.pallas_call(
        kernel,
        out_shape=(
            jax.ShapeDtypeStruct((2, 16, 512), F32),
            jax.ShapeDtypeStruct((64, 256), F32),
            jax.ShapeDtypeStruct((2, 256, 256), F32),
        ),
        in_specs=[whole] * 4,
        out_specs=[whole] * 3,
        scratch_shapes=scratch,
        compiler_params=pltpu.CompilerParams(
            collective_id=0, has_side_effects=True, vmem_limit_bytes=40 * 2 ** 20),
    )(boundary.reshape(2, 512, 256), gates_shared, gates_sliced[:, 0], cotangent[:, 0])
    amp, shared, sliced = pl.pallas_call(
        results,
        out_shape=(
            jax.ShapeDtypeStruct((2, 16, 512), F32),
            jax.ShapeDtypeStruct((64, 256), F32),
            jax.ShapeDtypeStruct((2, 256, 256), F32),
        ),
        in_specs=[whole] * 3,
        out_specs=[hbm] * 3,
        scratch_shapes=[pltpu.SemaphoreType.DMA((3,))],
        compiler_params=pltpu.CompilerParams(vmem_limit_bytes=8 * 2 ** 20),
    )(*parts)
    return amp[:, None], shared.reshape(2, 2, 16, 256), sliced[:, None]


def solution(mesh):
    return jax.shard_map(
        local,
        mesh=mesh,
        in_specs=(
            P(None, "cuts", "idx"),
            P(),
            P(None, "cuts", None, None),
            P(None, "idx", "cuts", None),
        ),
        out_specs=(
            P(None, "idx", "cuts", None),
            P(None, None, "cuts", None),
            P(None, "cuts", None, None),
        ),
        check_vma=False,
    )
```
